256 devices in a mesh: cuts: 8 (over y, core), rows: 32 (over x, z).
Axes of the slice: x: 4, y: 4, z: 8, core: 2. Of those that a mesh axis runs over, the one named last changes fastest.
Arguments:
- vectors: bfloat16 [65536, 1024], P('rows', 'cuts'), may hold values from -11.2 to 11.2
- blocks: bfloat16 [512, 8, 128, 128], P('rows'), may hold values from -0.1875 to 0.1875
- block_cols: int32 [512, 8], P('rows'), may hold values from 0 to 511, as said below
- counts: int32 [512], P('rows'), may hold values from 1 to 8, as said below
- lower_end: float32 [8], P('cuts'), may hold values from -2.4 to -1.9
- upper_end: float32 [8], P('cuts'), may hold values from 1.9 to 2.4
- coeffs: float32 [8, 7], P('cuts'), may hold values from -0.9 to 0.9
Outputs:
- projected: bfloat16 [65536, 1024], P('rows', 'cuts')
The draws below stay inside these ranges and needn't reach their ends.
Inputs may be any that keep to these rules, and one draw needn't show every extreme that they name: `block_cols`: slot 0 names the row block itself; the first counts of a row block's slots name distinct row blocks at most 4 away from it; later slots name the row block itself. The first row block of every group of 16 names the row block 4 below it, and the last the row block 4 above it, where those exist. `counts`: row blocks of some devices hold far more live slots than others; 8 is reached.
All inputs are finite; a program needn't handle non-finite values.
Results may differ from the reference program's by a relative error of at most 0.0065.
Values may be sent and summed in bfloat16 or wider, within the bound.
A program may use at most 64 MiB of HBM per device.

```python
import jax
import jax.numpy as jnp
import numpy as np
from jax import lax

BS = 128
NV = 128
NB = 32
MAXB = 8
W = 4
DEG = 6
PASSES = 2
RB_DEV = 16
NCUT = 8
NRB = 512
ORDER = 65536


def pattern(key):
    key = jax.random.fold_in(key, 11)
    k_shift, k_load, k_force, k_pick = jax.random.split(key, 4)
    dev_count = NRB // RB_DEV
    row_ids = jnp.arange(NRB, dtype=jnp.int32)
    device = row_ids // RB_DEV
    position = row_ids % RB_DEV
    shift_by = jax.random.randint(k_shift, (), 0, 4)
    forced_dev = jax.random.randint(k_force, (), 1, dev_count - 1)
    heavy_dev = ((device + shift_by) % 4 == 0) | (device == forced_dev)
    top_count = jnp.where(heavy_dev, MAXB, max(MAXB // 4, 1)).astype(jnp.int32)
    drawn_count = jax.random.randint(k_load, (NRB,), 0, 1 << 20) % top_count + 1
    forced_row = forced_dev * RB_DEV + RB_DEV // 2
    offsets = np.concatenate([np.arange(-W, 0), np.arange(1, W + 1)]).astype(np.int32)
    target = row_ids[:, None] + jnp.asarray(offsets)[None, :]
    in_range = (target >= 0) & (target < NRB)
    available = jnp.sum(in_range.astype(jnp.int32), axis=1)
    counts = jnp.minimum(drawn_count, available + 1)
    force_low = (position == 0) & (row_ids - W >= 0)
    force_high = (position == RB_DEV - 1) & (row_ids + W < NRB)
    needed = 1 + force_low.astype(jnp.int32) + force_high.astype(jnp.int32)
    counts = jnp.maximum(counts, needed)
    counts = jnp.where(row_ids == forced_row, MAXB, counts).astype(jnp.int32)
    spread = jnp.arange(2 * W, dtype=jnp.int32)[None, :]
    scores = jax.random.randint(k_pick, (NRB, 2 * W), 0, 1 << 16) * (2 * W) + spread
    top_score = (1 << 16) * (2 * W) + 2 * W
    scores = jnp.where(force_low[:, None] & (spread == 0), top_score, scores)
    scores = jnp.where(force_high[:, None] & (spread == 2 * W - 1), top_score + 1, scores)
    scores = jnp.where(in_range, scores, -1 - spread)
    ranked = jnp.argsort(-scores, axis=1)[:, :MAXB - 1]
    chosen = jnp.take_along_axis(target, ranked, axis=1)
    block_cols = jnp.concatenate([row_ids[:, None], chosen], axis=1)
    slot_ids = jnp.arange(MAXB, dtype=jnp.int32)
    block_cols = jnp.where(slot_ids[None, :] < counts[:, None], block_cols, row_ids[:, None])
    return (block_cols.astype(jnp.int32), counts)


def draw_block_cols(key, part):
    return pattern(key)[0]


def draw_counts(key, part):
    return pattern(key)[1]


def draw_vectors(key, part):
    k_base = jax.random.fold_in(key, 3)
    base_draw = jax.random.truncated_normal(k_base, -4.0, 4.0, (ORDER, NCUT, NV), jnp.float32)
    partner_cols = NV - NB + np.arange(NV) % NB
    partner = jnp.roll(base_draw, 1, axis=1)[:, :, partner_cols]
    amount = 0.2 + 1.6 * jnp.arange(ORDER, dtype=jnp.float32) / ORDER
    return (base_draw + amount[:, None, None] * partner).reshape(ORDER, NCUT * NV).astype(jnp.bfloat16)


def draw_coeffs(key, part):
    k_common, k_own = jax.random.split(jax.random.fold_in(key, 5))
    common = jax.random.uniform(k_common, (1, DEG + 1), jnp.float32, -0.6, 0.6)
    own_part = jax.random.uniform(k_own, (NCUT, DEG + 1), jnp.float32, -0.3, 0.3)
    return common + own_part


def shard_levels(own_key, dims, cuts, least, high):
    gain = 1.0
    for axis_at, parts in cuts:
        draws = jax.random.uniform(jax.random.fold_in(jax.random.fold_in(own_key, 6), axis_at), (parts,), jnp.float32, least / len(cuts), high / len(cuts))
        gain = gain * jnp.repeat(jnp.exp(draws), dims[axis_at] // parts).reshape((-1,) + (1,) * (len(dims) - 1 - axis_at))
    return gain


def normal_values(key, extent, deviation, limit, cuts=(), kind=jnp.bfloat16):
    loudness = shard_levels(key, extent, cuts, -0.22, 0.18) if cuts else 1.0
    drawn = jax.random.normal(key, extent, jnp.float32) * deviation * loudness
    return jnp.minimum(jnp.maximum(drawn, -limit), limit).astype(kind)


def setup_inputs(seed: int = 0) -> dict:
    key_of = jax.random.split(jax.random.key(seed), 8)
    return {
        "vectors": draw_vectors(jax.random.fold_in(key_of[7], 71), 0),
        "blocks": normal_values(key_of[1], (NRB, MAXB, BS, BS), (BS * MAXB) ** -0.5, 0.1875, ((0, 32),)),
        "block_cols": draw_block_cols(jax.random.fold_in(key_of[7], 71), 0),
        "counts": draw_counts(jax.random.fold_in(key_of[7], 71), 0),
        "lower_end": jnp.clip(-2.4 + 0.5000001 * jax.random.uniform(key_of[4], (NCUT,), jnp.float32) ** shard_levels(key_of[4], (NCUT,), ((0, 8),), -0.2, 0.2), -2.4, -1.9),
        "upper_end": jnp.clip(1.9 + 0.5000001 * jax.random.uniform(key_of[5], (NCUT,), jnp.float32) ** shard_levels(key_of[5], (NCUT,), ((0, 8),), -0.2, 0.2), 1.9, 2.4),
        "coeffs": draw_coeffs(jax.random.fold_in(key_of[7], 71), 0),
    }


def apply_matrix(blocks, block_cols, counts, rounded):
    row_blocks = blocks.shape[0]
    block_size = blocks.shape[2]
    tiles = lax.optimization_barrier(rounded).astype(jnp.float32).reshape(row_blocks, block_size, -1)
    summed = jnp.zeros(tiles.shape, jnp.float32)
    for slot_id in range(blocks.shape[1]):
        active = (counts > slot_id).astype(jnp.float32)
        tile_now = blocks[:, slot_id].astype(jnp.float32) * active[:, None, None]
        summed = summed + jnp.einsum('rij,rjv->riv', tile_now, tiles[block_cols[:, slot_id]])
    return summed.reshape(rounded.shape[0], -1)

def filter_pass(start, centre, half_width, weights, blocks, block_cols, counts):
    previous = start
    summed = weights[0] * previous
    product = apply_matrix(blocks, block_cols, counts, previous.astype(jnp.bfloat16))
    current = (product - centre * previous) / half_width
    summed = summed + weights[1] * current
    for term_k in range(2, DEG + 1):
        product = apply_matrix(blocks, block_cols, counts, current.astype(jnp.bfloat16))
        upcoming = 2.0 * (product - centre * current) / half_width - previous
        previous, current = (current, upcoming)
        summed = summed + weights[term_k] * current
    return summed

def reference(vectors, blocks, block_cols, counts, lower_end, upper_end, coeffs):
    groups = lower_end.shape[0]
    vec_cols = vectors.shape[1] // groups
    centre = jnp.repeat((lower_end + upper_end) * 0.5, vec_cols)
    half_width = jnp.repeat((upper_end - lower_end) * 0.5, vec_cols)
    weights = jnp.repeat(coeffs, vec_cols, axis=0).T
    filtered = vectors.astype(jnp.float32)
    for pass_id in range(PASSES):
        filtered = filter_pass(filtered, centre, half_width, weights, blocks, block_cols, counts)
    row_count = filtered.shape[0]
    grouped = filtered.reshape(row_count, groups, vec_cols)
    rounded_all = filtered.astype(jnp.bfloat16).reshape(row_count, groups, vec_cols)
    outputs = []
    for group in range(groups):
        own_cols = grouped[:, group]
        own_round = rounded_all[:, group]
        if group == 0:
            edge_vecs = jnp.zeros((row_count, NB), jnp.bfloat16)
        else:
            edge_vecs = rounded_all[:, group - 1, vec_cols - NB:]
        gram_sum = jnp.dot(edge_vecs.T.astype(jnp.float32), edge_vecs.astype(jnp.float32), preferred_element_type=jnp.float32) + jnp.eye(NB, dtype=jnp.float32)
        cross_sum = jnp.dot(edge_vecs.T.astype(jnp.float32), own_round.astype(jnp.float32), preferred_element_type=jnp.float32)
        factor = jnp.linalg.cholesky(gram_sum)
        solved = jax.scipy.linalg.cho_solve((factor, True), cross_sum).astype(jnp.bfloat16)
        outputs.append(own_cols - jnp.dot(edge_vecs.astype(jnp.float32), solved.astype(jnp.float32), preferred_element_type=jnp.float32))
    return jnp.stack(outputs, axis=1).reshape(row_count, -1).astype(jnp.bfloat16)
```

```python
import functools

import jax
import jax.numpy as jnp
from jax import lax
from jax.experimental import pallas as pl
from jax.experimental.pallas import tpu as pltpu
from jax.sharding import PartitionSpec as P

BS = 128
MAXB = 8
W = 4
DEG = 6
PASSES = 2
NB = 32
RB = 16
HALO = W * BS
OWN = RB * BS
QUADS = RB // W
WIDE = 3 * W * BS
MESH = pl.DeviceIdType.MESH
F32 = jnp.float32
BF16 = jnp.bfloat16


def dot(a, b):
    return jnp.dot(a, b, preferred_element_type=F32)


def tdot(a, b):
    return lax.dot_general(a, b, (((0,), (0,)), ((), ())), preferred_element_type=F32)


def kernel(
    nz,
    nx,
    ncut,
    vec,
    blocks,
    cols,
    counts,
    lower,
    upper,
    coeffs,
    out,
    stage0,
    stage1,
    stage2,
    stage3,
    dense,
    vbuf,
    ybuf,
    total,
    start,
    packed,
    arrived,
    acc,
    part,
    zin,
    xin,
    mid,
    full,
    block_sem,
    vec_sem,
    send_sem,
    recv_sem,
    edge_sem,
    zsend,
    zrecv,
    xsend,
    xrecv,
    gsend,
    grecv,
):
    stages = (stage0, stage1, stage2, stage3)
    row = lax.axis_index("rows")
    cut = lax.axis_index("cuts")
    nrow = nz * nx
    z = lax.rem(row, nz)
    x = lax.div(row, nz)
    low = lax.rem(row + nrow - 1, nrow)
    high = lax.rem(row + 1, nrow)
    after = lax.rem(cut + 1, ncut)
    before = lax.rem(cut + ncut - 1, ncut)
    zpeers = [x * nz + lax.rem(z + o, nz) for o in range(1, nz)]
    xpeers = [lax.rem(x + o, nx) * nz + z for o in range(1, nx)]

    vec_copy = pltpu.make_async_copy(vec, start, vec_sem)
    vec_copy.start()
    block_copies = []
    for q in range(QUADS):
        copy = pltpu.make_async_copy(
            blocks.at[pl.ds(q * W * MAXB, W * MAXB)],
            stages[q].at[pl.ds(0, W * MAXB)],
            block_sem.at[q],
        )
        copy.start()
        block_copies.append(copy)

    barrier = pltpu.get_barrier_semaphore()
    greeted = 0
    for other in [low, high, *zpeers, *xpeers]:
        pl.semaphore_signal(barrier, inc=1, device_id=(cut, other), device_id_type=MESH)
        greeted += 1
    for other in (before, after):
        pl.semaphore_signal(barrier, inc=1, device_id=(other, row), device_id_type=MESH)
        greeted += 1

    for q in range(QUADS):
        dense[q] = jnp.zeros((W * BS, WIDE), BF16)
        stages[q][W * MAXB] = jnp.zeros((BS, BS), BF16)
    centre = (lower[0] + upper[0]) * 0.5
    half = (upper[0] - lower[0]) * 0.5
    inverse = 1.0 / half

    pl.semaphore_wait(barrier, greeted)

    def to_low(src, slot):
        return pltpu.make_async_remote_copy(
            src_ref=src,
            dst_ref=vbuf.at[slot, pl.ds(HALO + OWN, HALO)],
            send_sem=send_sem.at[0, slot],
            recv_sem=recv_sem.at[1, slot],
            device_id=(cut, low),
            device_id_type=MESH,
        )

    def to_high(src, slot):
        return pltpu.make_async_remote_copy(
            src_ref=src,
            dst_ref=vbuf.at[slot, pl.ds(0, HALO)],
            send_sem=send_sem.at[1, slot],
            recv_sem=recv_sem.at[0, slot],
            device_id=(cut, high),
            device_id_type=MESH,
        )

    def low_edge(slot):
        return to_low(vbuf.at[slot, pl.ds(HALO, HALO)], slot)

    def high_edge(slot):
        return to_high(vbuf.at[slot, pl.ds(OWN, HALO)], slot)

    to_low(vec.at[pl.ds(0, HALO)], 0).start()
    to_high(vec.at[pl.ds(OWN - HALO, HALO)], 0).start()

    vec_copy.wait()
    vbuf[0, pl.ds(HALO, OWN)] = start[...]
    first = start[...].astype(F32)
    ybuf[0] = first
    ybuf[1] = jnp.zeros((OWN, BS), F32)
    total[...] = coeffs[0, 0] * first

    for q in range(QUADS):
        block_copies[q].wait()

        def place(i, carry, q=q):
            r = q * W + i
            base = row * RB + r - W
            live = counts[r]
            near = [jnp.where(s < live, cols[s, r] - base, -1) for s in range(MAXB)]
            for d in range(2 * W + 1):
                slot = jnp.int32(W * MAXB)
                for s in range(MAXB):
                    slot = jnp.where(near[s] == d, i * MAXB + s, slot)
                rows = pl.ds(pl.multiple_of(i * BS, BS), BS)
                lanes = pl.ds(pl.multiple_of((i + d) * BS, BS), BS)
                dense[q, rows, lanes] = stages[q][slot]
            return carry

        lax.fori_loop(0, W, place, 0)

    def step(k, carry):
        now = lax.rem(k, 2)
        new = 1 - now
        term = lax.rem(k, DEG)
        opening = term == 0
        closing = term == DEG - 1
        scale = jnp.where(opening, 1.0, 2.0) * inverse
        shift = scale * centre
        keep = jnp.where(opening, 0.0, 1.0)
        weight = coeffs[0, term + 1]
        first_weight = coeffs[0, 0]

        def finish(at, count, product):
            rows = pl.ds(at, count)
            upcoming = (
                scale * product - shift * ybuf[now, rows] - keep * ybuf[new, rows]
            )
            summed = total[rows] + weight * upcoming
            value = jnp.where(closing, summed, upcoming)
            total[rows] = jnp.where(closing, first_weight * summed, summed)
            ybuf[new, rows] = value
            vbuf[new, pl.ds(HALO + at, count)] = value.astype(BF16)

        half_rows = 2 * BS
        wide = (2 * W + 2) * BS
        def inner(n, carry):
            q, j = 1 + lax.div(n, 2), lax.rem(n, 2)
            at = pl.multiple_of(HALO + n * half_rows, half_rows)
            within = pl.multiple_of(j * half_rows, half_rows)
            product = dot(
                dense[q, pl.ds(within, half_rows), pl.ds(within, wide)],
                vbuf[now, pl.ds(at, wide)],
            )
            finish(at, half_rows, product)
            return carry

        lax.fori_loop(0, 4, inner, 0)
        acc[0] = dot(dense[0, :, HALO:], vbuf[now, pl.ds(HALO, 2 * HALO)])
        acc[1] = dot(dense[QUADS - 1, :, : 2 * HALO], vbuf[now, pl.ds(OWN - HALO, 2 * HALO)])

        @pl.when(k > 0)
        def _():
            low_edge(new).wait_send()
            high_edge(new).wait_send()

        to_high(vbuf.at[now, pl.ds(OWN, HALO)], now).wait_recv()
        finish(0, HALO, acc[0] + dot(dense[0, :, :HALO], vbuf[now, pl.ds(0, HALO)]))

        @pl.when(k < PASSES * DEG - 1)
        def _():
            low_edge(new).start()

        to_low(vbuf.at[now, pl.ds(HALO, HALO)], now).wait_recv()
        finish(
            OWN - HALO,
            HALO,
            acc[1] + dot(dense[QUADS - 1, :, 2 * HALO :], vbuf[now, pl.ds(HALO + OWN, HALO)]),
        )

        @pl.when(k < PASSES * DEG - 1)
        def _():
            high_edge(new).start()

        return carry

    lax.fori_loop(0, PASSES * DEG, step, 0)
    last = (PASSES * DEG) % 2
    low_edge(1 - last).wait_send()
    high_edge(1 - last).wait_send()

    lane = lax.broadcasted_iota(jnp.int32, (HALO, BS), 1)
    strip = jnp.zeros((HALO, BS), F32)
    for g in range(W):
        turned = pltpu.roll(ybuf[last, g * HALO : (g + 1) * HALO], (NB * (g + 1)) % BS, 1)
        strip = jnp.where(lane // NB == g, turned, strip)
    packed[...] = strip.astype(BF16)
    edge = pltpu.make_async_remote_copy(
        src_ref=packed,
        dst_ref=arrived,
        send_sem=edge_sem.at[0],
        recv_sem=edge_sem.at[1],
        device_id=(after, row),
        device_id_type=MESH,
    )
    edge.start()
    edge.wait()
    @pl.when(cut == 0)
    def _():
        arrived[...] = jnp.zeros((HALO, BS), BF16)

    boundary = arrived[...]
    cross = jnp.zeros((NB, BS), F32)
    for g in range(W):
        mine = vbuf[last, pl.ds(HALO + g * HALO, HALO)]
        cross = cross + tdot(boundary, mine)[g * NB : (g + 1) * NB]
    square = tdot(boundary, boundary)
    gram = jnp.zeros((NB, BS), F32)
    for g in range(W):
        rows = square[g * NB : (g + 1) * NB]
        gram = gram + (pltpu.roll(rows, (BS - NB * g) % BS, 1) if g else rows)
    part[0:NB] = cross
    part[NB : 2 * NB] = gram

    piece = 2 * NB // nz
    mine = pl.ds(pl.multiple_of(z * piece, piece), piece)
    copies = []
    for o in range(1, nz):
        theirs = pl.multiple_of(lax.rem(z + o, nz) * piece, piece)
        copies.append(
            pltpu.make_async_remote_copy(
                src_ref=part.at[pl.ds(theirs, piece)],
                dst_ref=zin.at[o - 1],
                send_sem=zsend.at[o - 1],
                recv_sem=zrecv.at[o - 1],
                device_id=(cut, zpeers[o - 1]),
                device_id_type=MESH,
            )
        )
        copies[-1].start()
    summed = part[mine]
    for o in range(1, nz):
        copies[o - 1].wait()
        summed = summed + zin[o - 1]
    mid[...] = summed
    copies = []
    for o in range(1, nx):
        copies.append(
            pltpu.make_async_remote_copy(
                src_ref=mid,
                dst_ref=xin.at[o - 1],
                send_sem=xsend.at[o - 1],
                recv_sem=xrecv.at[o - 1],
                device_id=(cut, xpeers[o - 1]),
                device_id_type=MESH,
            )
        )
        copies[-1].start()
    for o in range(1, nx):
        copies[o - 1].wait()
        summed = summed + xin[o - 1]
    full[mine] = summed
    copies = []
    for o in range(1, nz):
        copies.append(
            pltpu.make_async_remote_copy(
                src_ref=full.at[mine],
                dst_ref=full.at[mine],
                send_sem=gsend.at[o - 1],
                recv_sem=grecv.at[o - 1],
                device_id=(cut, zpeers[o - 1]),
                device_id_type=MESH,
            )
        )
        copies[-1].start()
    for copy in copies:
        copy.wait()

    across = lax.broadcasted_iota(jnp.int32, (NB, BS), 1)
    down = lax.broadcasted_iota(jnp.int32, (NB, BS), 0)
    right = full[0:NB]
    left = full[NB : 2 * NB] + jnp.where(across == down, 1.0, 0.0)
    for j in range(NB):
        column = left[:, j : j + 1]
        pivot = 1.0 / left[j : j + 1, j : j + 1]
        lrow = left[j : j + 1] * pivot
        rrow = right[j : j + 1] * pivot
        left = jnp.where(down == j, lrow, left - column * lrow)
        right = jnp.where(down == j, rrow, right - column * rrow)
    solved = right.astype(BF16).astype(F32)
    for g in range(W):
        above_rows = [jnp.zeros((NB, BS), F32)] * g
        below_rows = [jnp.zeros((NB, BS), F32)] * (W - 1 - g)
        spread = jnp.concatenate([*above_rows, solved, *below_rows], axis=0).astype(BF16)
        correction = dot(boundary, spread)
        rows = pl.ds(g * HALO, HALO)
        out[rows] = (ybuf[last, rows] - correction).astype(BF16)


def body(nz, nx, ncut, vectors, blocks, block_cols, counts, lower_end, upper_end, coeffs):
    blocks = blocks.reshape(RB * MAXB, BS, BS)
    hbm = pl.BlockSpec(memory_space=pl.ANY)
    smem = pl.BlockSpec(memory_space=pltpu.SMEM)
    stage = pltpu.VMEM((W * MAXB + 1, BS, BS), BF16)
    dma = pltpu.SemaphoreType.DMA
    piece = 2 * NB // nz
    return pl.pallas_call(
        functools.partial(kernel, nz, nx, ncut),
        out_shape=jax.ShapeDtypeStruct((OWN, BS), BF16),
        in_specs=[hbm, hbm, smem, smem, smem, smem, smem],
        out_specs=pl.BlockSpec(memory_space=pltpu.VMEM),
        scratch_shapes=[
            stage,
            stage,
            stage,
            stage,
            pltpu.VMEM((QUADS, HALO, WIDE), BF16),
            pltpu.VMEM((2, OWN + 2 * HALO, BS), BF16),
            pltpu.VMEM((2, OWN, BS), F32),
            pltpu.VMEM((OWN, BS), F32),
            pltpu.VMEM((OWN, BS), BF16),
            pltpu.VMEM((HALO, BS), BF16),
            pltpu.VMEM((HALO, BS), BF16),
            pltpu.VMEM((2, HALO, BS), F32),
            pltpu.VMEM((2 * NB, BS), F32),
            pltpu.VMEM((nz - 1, piece, BS), F32),
            pltpu.VMEM((nx - 1, piece, BS), F32),
            pltpu.VMEM((piece, BS), F32),
            pltpu.VMEM((2 * NB, BS), F32),
            dma((QUADS,)),
            dma,
            dma((2, 2)),
            dma((2, 2)),
            dma((2,)),
            dma((nz - 1,)),
            dma((nz - 1,)),
            dma((nx - 1,)),
            dma((nx - 1,)),
            dma((nz - 1,)),
            dma((nz - 1,)),
        ],
        compiler_params=pltpu.CompilerParams(
            collective_id=0, has_side_effects=True, vmem_limit_bytes=60 * 1024 * 1024
        ),
    )(vectors, blocks, block_cols.T, counts, lower_end, upper_end, coeffs)


def solution(mesh):
    rows = mesh.shape["rows"]
    nx = 4 if rows == 32 else 2
    return jax.shard_map(
        functools.partial(body, rows // nx, nx, mesh.shape["cuts"]),
        mesh=mesh,
        in_specs=(
            P("rows", "cuts"),
            P("rows", None, None, None),
            P("rows", None),
            P("rows"),
            P("cuts"),
            P("cuts"),
            P("cuts", None),
        ),
        out_specs=P("rows", "cuts"),
        check_vma=False,
    )
```

```python
import functools

import jax
import jax.numpy as jnp
from jax import lax
from jax.experimental import pallas as pl
from jax.experimental.pallas import tpu as pltpu
from jax.sharding import PartitionSpec as P

BS = 128
MAXB = 8
W = 4
DEG = 6
PASSES = 2
NB = 32
RB = 16
HALO = W * BS
PIECE = HALO // 2
OWN = RB * BS
QUADS = RB // W
WIDE = 3 * W * BS
MESH = pl.DeviceIdType.MESH
F32 = jnp.float32
BF16 = jnp.bfloat16


def dot(a, b):
    return jnp.dot(a, b, preferred_element_type=F32)


def tdot(a, b):
    return lax.dot_general(a, b, (((0,), (0,)), ((), ())), preferred_element_type=F32)


def kernel(
    nz,
    nx,
    ncut,
    vec,
    blocks,
    cols_in,
    counts_in,
    lower_in,
    upper_in,
    coeffs_in,
    out,
    cols,
    counts,
    lower,
    upper,
    coeffs,
    stage0,
    stage1,
    stage2,
    stage3,
    dense,
    vbuf,
    ybuf,
    total,
    start,
    packed,
    arrived,
    acc,
    gpart,
    gzin,
    gmid,
    gxin,
    cpart,
    czin,
    cmid,
    cxin,
    small_sem,
    block_sem,
    vec_sem,
    send_sem,
    recv_sem,
    edge_sem,
    gzsend,
    gzrecv,
    gxsend,
    gxrecv,
    czsend,
    czrecv,
    cxsend,
    cxrecv,
):
    stages = (stage0, stage1, stage2, stage3)
    row = lax.axis_index("rows")
    cut = lax.axis_index("cuts")
    nrow = nz * nx
    z = lax.rem(row, nz)
    x = lax.div(row, nz)
    low = lax.rem(row + nrow - 1, nrow)
    high = lax.rem(row + 1, nrow)
    after = lax.rem(cut + 1, ncut)
    before = lax.rem(cut + ncut - 1, ncut)
    zpeers = [x * nz + lax.rem(z + o, nz) for o in range(1, nz)]
    xpeers = [lax.rem(x + o, nx) * nz + z for o in range(1, nx)]

    vec_copy = pltpu.make_async_copy(vec, start, vec_sem)
    vec_copy.start()
    small = []
    for n, (src, dst) in enumerate(
        ((lower_in, lower), (upper_in, upper), (coeffs_in, coeffs), (cols_in, cols), (counts_in, counts))
    ):
        small.append(pltpu.make_async_copy(src, dst, small_sem.at[n]))
        small[-1].start()
    block_copies = []
    for q in range(QUADS):
        copy = pltpu.make_async_copy(
            blocks.at[pl.ds(q * W * MAXB, W * MAXB)],
            stages[q].at[pl.ds(0, W * MAXB)],
            block_sem.at[q],
        )
        copy.start()
        block_copies.append(copy)

    barrier = pltpu.get_barrier_semaphore()
    greeted = 0
    for other in [low, high, *zpeers, *xpeers]:
        pl.semaphore_signal(barrier, inc=1, device_id=(cut, other), device_id_type=MESH)
        greeted += 1
    for other in (before, after):
        pl.semaphore_signal(barrier, inc=1, device_id=(other, row), device_id_type=MESH)
        greeted += 1

    for q in range(QUADS):
        dense[q] = jnp.zeros((W * BS, WIDE), BF16)
        stages[q][W * MAXB] = jnp.zeros((BS, BS), BF16)
    for copy in small:
        copy.wait()
    centre = (lower[0] + upper[0]) * 0.5
    half = (upper[0] - lower[0]) * 0.5
    inverse = 1.0 / half

    pl.semaphore_wait(barrier, greeted)

    def to_low(src, slot, p):
        return pltpu.make_async_remote_copy(
            src_ref=src,
            dst_ref=vbuf.at[slot, pl.ds(HALO + OWN + p * PIECE, PIECE)],
            send_sem=send_sem.at[0, slot, p],
            recv_sem=recv_sem.at[1, slot, p],
            device_id=(cut, low),
            device_id_type=MESH,
        )

    def to_high(src, slot, p):
        return pltpu.make_async_remote_copy(
            src_ref=src,
            dst_ref=vbuf.at[slot, pl.ds(p * PIECE, PIECE)],
            send_sem=send_sem.at[1, slot, p],
            recv_sem=recv_sem.at[0, slot, p],
            device_id=(cut, high),
            device_id_type=MESH,
        )

    def low_edge(slot, p):
        return to_low(vbuf.at[slot, pl.ds(HALO + p * PIECE, PIECE)], slot, p)

    def high_edge(slot, p):
        return to_high(vbuf.at[slot, pl.ds(OWN + p * PIECE, PIECE)], slot, p)

    for p in (0, 1):
        to_high(vec.at[pl.ds(OWN - HALO + p * PIECE, PIECE)], 0, p).start()
        to_low(vec.at[pl.ds(p * PIECE, PIECE)], 0, p).start()

    vec_copy.wait()
    vbuf[0, pl.ds(HALO, OWN)] = start[...]
    first = start[...].astype(F32)
    ybuf[0] = first
    ybuf[1] = jnp.zeros((OWN, BS), F32)
    total[...] = coeffs[0, 0] * first

    for q in range(QUADS):
        block_copies[q].wait()

        def place(i, carry, q=q):
            r = q * W + i
            base = row * RB + r - W
            live = counts[r]
            near = [jnp.where(s < live, cols[s, r] - base, -1) for s in range(MAXB)]
            for d in range(2 * W + 1):
                slot = jnp.int32(W * MAXB)
                for s in range(MAXB):
                    slot = jnp.where(near[s] == d, i * MAXB + s, slot)
                rows = pl.ds(pl.multiple_of(i * BS, BS), BS)
                lanes = pl.ds(pl.multiple_of((i + d) * BS, BS), BS)
                dense[q, rows, lanes] = stages[q][slot]
            return carry

        lax.fori_loop(0, W, place, 0)

    def step(k, carry):
        now = lax.rem(k, 2)
        new = 1 - now
        term = lax.rem(k, DEG)
        opening = term == 0
        closing = term == DEG - 1
        scale = jnp.where(opening, 1.0, 2.0) * inverse
        shift = scale * centre
        keep = jnp.where(opening, 0.0, 1.0)
        weight = coeffs[0, term + 1]
        first_weight = coeffs[0, 0]

        def finish(at, count, product):
            rows = pl.ds(at, count)
            upcoming = (
                scale * product - shift * ybuf[now, rows] - keep * ybuf[new, rows]
            )
            summed = total[rows] + weight * upcoming
            value = jnp.where(closing, summed, upcoming)
            total[rows] = jnp.where(closing, first_weight * summed, summed)
            ybuf[new, rows] = value
            vbuf[new, pl.ds(HALO + at, count)] = value.astype(BF16)

        half_rows = 2 * BS
        wide = (2 * W + 2) * BS
        def inner(n, carry):
            q, j = 1 + lax.div(n, 2), lax.rem(n, 2)
            at = pl.multiple_of(HALO + n * half_rows, half_rows)
            within = pl.multiple_of(j * half_rows, half_rows)
            product = dot(
                dense[q, pl.ds(within, half_rows), pl.ds(within, wide)],
                vbuf[now, pl.ds(at, wide)],
            )
            finish(at, half_rows, product)
            return carry

        lax.fori_loop(0, 4, inner, 0)
        acc[0] = dot(dense[0, :, HALO:], vbuf[now, pl.ds(HALO, 2 * HALO)])
        acc[1] = dot(dense[QUADS - 1, :, : 2 * HALO], vbuf[now, pl.ds(OWN - HALO, 2 * HALO)])

        @pl.when(k > 0)
        def _():
            for p in (0, 1):
                low_edge(new, p).wait_send()
                high_edge(new, p).wait_send()

        more = k < PASSES * DEG - 1
        for p in (0, 1):
            low_edge(now, p).wait_recv()
            inside = slice(p * PIECE, (p + 1) * PIECE)
            deep = (p + 1) * PIECE
            finish(
                OWN - HALO + p * PIECE,
                PIECE,
                acc[1, inside]
                + dot(dense[QUADS - 1, inside, 2 * HALO : 2 * HALO + deep], vbuf[now, pl.ds(HALO + OWN, deep)]),
            )

            @pl.when(more)
            def _(p=p):
                high_edge(new, p).start()

        for p in (0, 1):
            high_edge(now, p).wait_recv()
        for p in (0, 1):
            inside = slice(p * PIECE, (p + 1) * PIECE)
            finish(
                p * PIECE,
                PIECE,
                acc[0, inside] + dot(dense[0, inside, p * PIECE : HALO], vbuf[now, pl.ds(p * PIECE, HALO - p * PIECE)]),
            )

            @pl.when(more)
            def _(p=p):
                low_edge(new, p).start()

        return carry

    lax.fori_loop(0, PASSES * DEG, step, 0)
    last = (PASSES * DEG) % 2
    for p in (0, 1):
        low_edge(1 - last, p).wait_send()
        high_edge(1 - last, p).wait_send()

    lane = lax.broadcasted_iota(jnp.int32, (HALO, BS), 1)
    strip = jnp.zeros((HALO, BS), F32)
    for g in range(W):
        turned = pltpu.roll(ybuf[last, g * HALO : (g + 1) * HALO], (NB * (g + 1)) % BS, 1)
        strip = jnp.where(lane // NB == g, turned, strip)
    packed[...] = strip.astype(BF16)
    edge = pltpu.make_async_remote_copy(
        src_ref=packed,
        dst_ref=arrived,
        send_sem=edge_sem.at[0],
        recv_sem=edge_sem.at[1],
        device_id=(after, row),
        device_id_type=MESH,
    )
    edge.start()
    edge.wait()
    @pl.when(cut == 0)
    def _():
        arrived[...] = jnp.zeros((HALO, BS), BF16)

    def share(src, slots, sent, got, peers):
        copies = []
        for o, peer in enumerate(peers):
            copies.append(
                pltpu.make_async_remote_copy(
                    src_ref=src,
                    dst_ref=slots.at[o],
                    send_sem=sent.at[o],
                    recv_sem=got.at[o],
                    device_id=(cut, peer),
                    device_id_type=MESH,
                )
            )
            copies[-1].start()
        return copies

    def collect(copies, own, slots):
        summed = own
        for o, copy in enumerate(copies):
            copy.wait()
            summed = summed + slots[o]
        return summed

    boundary = arrived[...]
    square = tdot(boundary, boundary)
    eight = BS // W // W
    group = lax.broadcasted_iota(jnp.int32, (eight, BS), 1) // NB
    gram = jnp.zeros((NB, BS), F32)
    for g in range(W):
        rows = square[g * NB : (g + 1) * NB]
        gram = gram + (pltpu.roll(rows, (BS - NB * g) % BS, 1) if g else rows)
    tight = jnp.zeros((eight, BS), F32)
    for g in range(W):
        rows = gram[g * eight : (g + 1) * eight]
        tight = jnp.where(group == g, pltpu.roll(rows, NB * g, 1) if g else rows, tight)
    gpart[...] = tight
    gram_z = share(gpart, gzin, gzsend, gzrecv, zpeers)
    cross = jnp.zeros((NB, BS), F32)
    for g in range(W):
        mine = vbuf[last, pl.ds(HALO + g * HALO, HALO)]
        cross = cross + tdot(boundary, mine)[g * NB : (g + 1) * NB]
    cpart[...] = cross
    cross_z = share(cpart, czin, czsend, czrecv, zpeers)
    gmid[...] = collect(gram_z, tight, gzin)
    gram_x = share(gmid, gxin, gxsend, gxrecv, xpeers)
    cmid[...] = collect(cross_z, cross, czin)
    cross_x = share(cmid, cxin, cxsend, cxrecv, xpeers)
    tight = collect(gram_x, gmid[...], gxin)

    across = lax.broadcasted_iota(jnp.int32, (NB, BS), 1)
    down = lax.broadcasted_iota(jnp.int32, (NB, BS), 0)
    loose = [tight if g == 0 else pltpu.roll(tight, BS - NB * g, 1) for g in range(W)]
    whole = jnp.where(across < NB, jnp.concatenate(loose, axis=0), 0.0)
    whole = whole + jnp.where((across == down) | (across == down + NB), 1.0, 0.0)
    for j in range(NB):
        row_j = whole[j : j + 1] * (1.0 / whole[j : j + 1, j : j + 1])
        whole = jnp.where(down == j, row_j, whole - whole[:, j : j + 1] * row_j)
    summed = collect(cross_x, cmid[...], cxin)
    tall = jnp.concatenate(
        [jnp.zeros((NB, BS), F32), summed, jnp.zeros((2 * NB, BS), F32)], axis=0
    )
    right = jnp.dot(whole, tall, preferred_element_type=F32, precision=lax.Precision.HIGHEST)
    solved = right.astype(BF16).astype(F32)
    for g in range(W):
        above_rows = [jnp.zeros((NB, BS), F32)] * g
        below_rows = [jnp.zeros((NB, BS), F32)] * (W - 1 - g)
        spread = jnp.concatenate([*above_rows, solved, *below_rows], axis=0).astype(BF16)
        correction = dot(boundary, spread)
        rows = pl.ds(g * HALO, HALO)
        out[rows] = (ybuf[last, rows] - correction).astype(BF16)


def body(nz, nx, ncut, vectors, blocks, block_cols, counts, lower_end, upper_end, coeffs):
    blocks = blocks.reshape(RB * MAXB, BS, BS)
    hbm = pl.BlockSpec(memory_space=pltpu.HBM)
    stage = pltpu.VMEM((W * MAXB + 1, BS, BS), BF16)
    dma = pltpu.SemaphoreType.DMA
    return pl.pallas_call(
        functools.partial(kernel, nz, nx, ncut),
        out_shape=jax.ShapeDtypeStruct((OWN, BS), BF16),
        in_specs=[hbm] * 7,
        out_specs=pl.BlockSpec(memory_space=pltpu.VMEM),
        scratch_shapes=[
            pltpu.SMEM((MAXB, RB), jnp.int32),
            pltpu.SMEM((RB,), jnp.int32),
            pltpu.SMEM((1,), F32),
            pltpu.SMEM((1,), F32),
            pltpu.SMEM((1, DEG + 1), F32),
            stage,
            stage,
            stage,
            stage,
            pltpu.VMEM((QUADS, HALO, WIDE), BF16),
            pltpu.VMEM((2, OWN + 2 * HALO, BS), BF16),
            pltpu.VMEM((2, OWN, BS), F32),
            pltpu.VMEM((OWN, BS), F32),
            pltpu.VMEM((OWN, BS), BF16),
            pltpu.VMEM((HALO, BS), BF16),
            pltpu.VMEM((HALO, BS), BF16),
            pltpu.VMEM((2, HALO, BS), F32),
            pltpu.VMEM((8, BS), F32),
            pltpu.VMEM((nz - 1, 8, BS), F32),
            pltpu.VMEM((8, BS), F32),
            pltpu.VMEM((nx - 1, 8, BS), F32),
            pltpu.VMEM((NB, BS), F32),
            pltpu.VMEM((nz - 1, NB, BS), F32),
            pltpu.VMEM((NB, BS), F32),
            pltpu.VMEM((nx - 1, NB, BS), F32),
            dma((5,)),
            dma((QUADS,)),
            dma,
            dma((2, 2, 2)),
            dma((2, 2, 2)),
            dma((2,)),
            *[dma((n,)) for n in 2 * [nz - 1, nz - 1, nx - 1, nx - 1]],
        ],
        compiler_params=pltpu.CompilerParams(
            collective_id=0, has_side_effects=True, vmem_limit_bytes=60 * 1024 * 1024
        ),
    )(vectors, blocks, block_cols.T, counts, lower_end, upper_end, coeffs)


def solution(mesh):
    rows = mesh.shape["rows"]
    nx = 4 if rows == 32 else 2
    return jax.shard_map(
        functools.partial(body, rows // nx, nx, mesh.shape["cuts"]),
        mesh=mesh,
        in_specs=(
            P("rows", "cuts"),
            P("rows", None, None, None),
            P("rows", None),
            P("rows"),
            P("cuts"),
            P("cuts"),
            P("cuts", None),
        ),
        out_specs=P("rows", "cuts"),
        check_vma=False,
    )
```

```python
import functools

import jax
import jax.numpy as jnp
from jax import lax
from jax.experimental import pallas as pl
from jax.experimental.pallas import tpu as pltpu
from jax.sharding import PartitionSpec as P

BS = 128
MAXB = 8
W = 4
DEG = 6
PASSES = 2
NB = 32
RB = 16
HALO = W * BS
NP = 4
PIECE = HALO // NP
ROUNDS = PASSES * DEG // 2
OWN = RB * BS
QUADS = RB // W
WIDE = 3 * W * BS
MESH = pl.DeviceIdType.MESH
F32 = jnp.float32
BF16 = jnp.bfloat16


def dot(a, b):
    return jnp.dot(a, b, preferred_element_type=F32)


def tdot(a, b):
    return lax.dot_general(a, b, (((0,), (0,)), ((), ())), preferred_element_type=F32)


def kernel(
    nz,
    nx,
    ncut,
    vec,
    blocks,
    cols_in,
    counts_in,
    lower_in,
    upper_in,
    coeffs_in,
    out,
    cols,
    counts,
    lower,
    upper,
    coeffs,
    stage0,
    stage1,
    stage2,
    stage3,
    dense,
    vbuf,
    ybuf,
    total,
    start,
    packed,
    arrived,
    acc,
    halo,
    ahead,
    fetched,
    known,
    middle,
    corner,
    gpart,
    gzin,
    gmid,
    gxin,
    cpart,
    czin,
    cmid,
    cxin,
    small_sem,
    block_sem,
    vec_sem,
    send_sem,
    recv_sem,
    asend,
    arecv,
    csem,
    edge_sem,
    gzsend,
    gzrecv,
    gxsend,
    gxrecv,
    czsend,
    czrecv,
    cxsend,
    cxrecv,
):
    stages = (stage0, stage1, stage2, stage3)
    row = lax.axis_index("rows")
    cut = lax.axis_index("cuts")
    nrow = nz * nx
    z = lax.rem(row, nz)
    x = lax.div(row, nz)
    low = lax.rem(row + nrow - 1, nrow)
    high = lax.rem(row + 1, nrow)
    after = lax.rem(cut + 1, ncut)
    before = lax.rem(cut + ncut - 1, ncut)
    zpeers = [x * nz + lax.rem(z + o, nz) for o in range(1, nz)]
    xpeers = [lax.rem(x + o, nx) * nz + z for o in range(1, nx)]

    vec_copy = pltpu.make_async_copy(vec, start, vec_sem)
    vec_copy.start()
    small = []
    for n, (src, dst) in enumerate(
        ((lower_in, lower), (upper_in, upper), (coeffs_in, coeffs), (cols_in, cols), (counts_in, counts))
    ):
        small.append(pltpu.make_async_copy(src, dst, small_sem.at[n]))
        small[-1].start()
    block_copies = []
    for q in range(QUADS):
        copy = pltpu.make_async_copy(
            blocks.at[pl.ds(q * W * MAXB, W * MAXB)],
            stages[q].at[pl.ds(0, W * MAXB)],
            block_sem.at[q],
        )
        copy.start()
        block_copies.append(copy)

    barrier = pltpu.get_barrier_semaphore()
    greeted = 0
    for other in [low, high, *zpeers, *xpeers]:
        pl.semaphore_signal(barrier, inc=1, device_id=(cut, other), device_id_type=MESH)
        greeted += 1
    for other in (before, after):
        pl.semaphore_signal(barrier, inc=1, device_id=(other, row), device_id_type=MESH)
        greeted += 1

    for q in range(QUADS):
        dense[q] = jnp.zeros((W * BS, WIDE), BF16)
        stages[q][W * MAXB] = jnp.zeros((BS, BS), BF16)
    for copy in small:
        copy.wait()
    centre = (lower[0] + upper[0]) * 0.5
    half = (upper[0] - lower[0]) * 0.5
    inverse = 1.0 / half

    pl.semaphore_wait(barrier, greeted)

    def side_copy(src, dst, sent, got, device):
        return pltpu.make_async_remote_copy(
            src_ref=src,
            dst_ref=dst,
            send_sem=sent,
            recv_sem=got,
            device_id=(cut, device),
            device_id_type=MESH,
        )

    def to_low(src, turn, p):
        return side_copy(
            src,
            halo.at[turn, 1, pl.ds(p * PIECE, PIECE)],
            send_sem.at[0, turn, p],
            recv_sem.at[1, turn, p],
            low,
        )

    def to_high(src, turn, p):
        return side_copy(
            src,
            halo.at[turn, 0, pl.ds(p * PIECE, PIECE)],
            send_sem.at[1, turn, p],
            recv_sem.at[0, turn, p],
            high,
        )

    def low_edge(slot, turn, p):
        return to_low(vbuf.at[slot, pl.ds(p * PIECE, PIECE)], turn, p)

    def high_edge(slot, turn, p):
        return to_high(vbuf.at[slot, pl.ds(OWN - HALO + p * PIECE, PIECE)], turn, p)

    def low_ahead(turn, p):
        at = pl.ds(p * PIECE, PIECE)
        return side_copy(
            ahead.at[0, at],
            fetched.at[turn, 1, at],
            asend.at[0, turn, p],
            arecv.at[1, turn, p],
            low,
        )

    def high_ahead(turn, p):
        at = pl.ds(p * PIECE, PIECE)
        return side_copy(
            ahead.at[1, at],
            fetched.at[turn, 0, at],
            asend.at[1, turn, p],
            arecv.at[0, turn, p],
            high,
        )

    low_corner = side_copy(
        dense.at[0, :, pl.ds(0, HALO)], corner.at[1], csem.at[0, 0], csem.at[1, 1], low
    )
    high_corner = side_copy(
        dense.at[QUADS - 1, :, pl.ds(2 * HALO, HALO)],
        corner.at[0],
        csem.at[0, 1],
        csem.at[1, 0],
        high,
    )

    for p in range(NP):
        to_high(vec.at[pl.ds(OWN - HALO + p * PIECE, PIECE)], 0, p).start()
        to_low(vec.at[pl.ds(p * PIECE, PIECE)], 0, p).start()

    vec_copy.wait()
    vbuf[0] = start[...]
    first = start[...].astype(F32)
    ybuf[0] = first
    ybuf[1] = jnp.zeros((OWN, BS), F32)
    total[...] = coeffs[0, 0] * first

    for q in range(QUADS):
        block_copies[q].wait()

        def place(i, carry, q=q):
            r = q * W + i
            base = row * RB + r - W
            live = counts[r]
            near = [jnp.where(s < live, cols[s, r] - base, -1) for s in range(MAXB)]
            for d in range(2 * W + 1):
                slot = jnp.int32(W * MAXB)
                for s in range(MAXB):
                    slot = jnp.where(near[s] == d, i * MAXB + s, slot)
                rows = pl.ds(pl.multiple_of(i * BS, BS), BS)
                lanes = pl.ds(pl.multiple_of((i + d) * BS, BS), BS)
                dense[q, rows, lanes] = stages[q][slot]
            return carry

        lax.fori_loop(0, W, place, 0)

    low_corner.start()
    high_corner.start()

    def factors(term):
        opening = term == 0
        scale = jnp.where(opening, 1.0, 2.0) * inverse
        return scale, scale * centre, jnp.where(opening, 0.0, 1.0)

    def recur(now, new, rows, product, scales):
        scale, shift, keep = scales
        return scale * product - shift * ybuf[now, rows] - keep * ybuf[new, rows]

    def settle(new, rows, upcoming, term):
        closing = term == DEG - 1
        summed = total[rows] + coeffs[0, term + 1] * upcoming
        value = jnp.where(closing, summed, upcoming)
        total[rows] = jnp.where(closing, coeffs[0, 0] * summed, summed)
        ybuf[new, rows] = value
        vbuf[new, rows] = value.astype(BF16)

    def inner(now, new, term, scales):
        pair = 2 * BS
        wide = (2 * W + 2) * BS
        for q in (1, 2):
            for j in (0, 1):
                at = q * HALO + j * pair
                product = dot(
                    dense[q, j * pair : (j + 1) * pair, j * pair : j * pair + wide],
                    vbuf[now, pl.ds(at - HALO, wide)],
                )
                rows = pl.ds(at, pair)
                settle(new, rows, recur(now, new, rows, product, scales), term)

    top, bottom = pl.ds(0, HALO), pl.ds(OWN - HALO, HALO)

    def own_part(now, new, scales):
        product = dot(dense[QUADS - 1, :, : 2 * HALO], vbuf[now, pl.ds(OWN - 2 * HALO, 2 * HALO)])
        acc[1] = recur(now, new, bottom, product, scales)
        product = dot(dense[0, :, HALO:], vbuf[now, pl.ds(0, 2 * HALO)])
        acc[0] = recur(now, new, top, product, scales)

    def bottom_piece(src, p, scales):
        inside = slice(p * PIECE, (p + 1) * PIECE)
        deep = (p + 1) * PIECE
        product = dot(dense[QUADS - 1, inside, 2 * HALO : 2 * HALO + deep], src[pl.ds(0, deep)])
        return acc[1, inside] + scales[0] * product

    def top_piece(src, p, scales):
        inside = slice(p * PIECE, (p + 1) * PIECE)
        product = dot(
            dense[0, inside, p * PIECE : HALO], src[pl.ds(p * PIECE, HALO - p * PIECE)]
        )
        return acc[0, inside] + scales[0] * product

    def edges(new, turn):
        return [f(new, turn, p) for f in (high_edge, low_edge) for p in range(NP)]

    def step(k, carry):
        now = lax.rem(k, 2)
        new = 1 - now
        scales = factors(k)
        own_part(now, new, scales)
        inner(now, new, k, scales)

        @pl.when(k > 0)
        def _():
            for copy in edges(new, new):
                copy.wait_send()

        for p in range(NP):
            low_edge(now, now, p).wait_recv()
            settle(
                new,
                pl.ds(OWN - HALO + p * PIECE, PIECE),
                bottom_piece(halo.at[now, 1], p, scales),
                k,
            )
            high_edge(new, new, p).start()
        for p in range(NP):
            high_edge(now, now, p).wait_recv()
        for p in range(NP):
            settle(new, pl.ds(p * PIECE, PIECE), top_piece(halo.at[now, 0], p, scales), k)
            low_edge(new, new, p).start()
        return carry

    lax.fori_loop(0, 2, step, 0)
    low_corner.wait()
    high_corner.wait()
    for copy in edges(1, 1):
        copy.wait_send()

    def double(j, carry):
        turn = lax.rem(j + 1, 2)
        later = 1 - turn
        term = lax.rem(2 * j, DEG)
        scales = factors(term)

        @pl.when(j > 1)
        def _():
            for p in range(NP):
                low_ahead(later, p).wait_send()
                high_ahead(later, p).wait_send()

        own_part(0, 1, scales)
        ahead[1] = acc[1].astype(BF16)
        for p in range(NP):
            high_ahead(turn, p).start()
        ahead[0] = acc[0].astype(BF16)
        for p in range(NP):
            low_ahead(turn, p).start()
        known[1] = scales[0] * dot(corner[1], vbuf[0, bottom])
        known[0] = scales[0] * dot(corner[0], vbuf[0, top])
        inner(0, 1, term, scales)
        for p in range(NP):
            low_edge(0, turn, p).wait_recv()
        for p in range(NP):
            rows = pl.ds(OWN - HALO + p * PIECE, PIECE)
            settle(1, rows, bottom_piece(halo.at[turn, 1], p, scales), term)
        for p in range(NP):
            high_edge(0, turn, p).wait_recv()
        for p in range(NP):
            rows = pl.ds(p * PIECE, PIECE)
            settle(1, rows, top_piece(halo.at[turn, 0], p, scales), term)

        for copy in edges(0, turn):
            copy.wait_send()
        scales = factors(term + 1)
        own_part(1, 0, scales)
        inner(1, 0, term + 1, scales)
        more = j < ROUNDS - 1
        for p in range(NP):
            low_ahead(turn, p).wait_recv()
            at = pl.ds(p * PIECE, PIECE)
            middle[1, at] = (fetched[turn, 1, at].astype(F32) + known[1, at]).astype(BF16)
            rows = pl.ds(OWN - HALO + p * PIECE, PIECE)
            settle(0, rows, bottom_piece(middle.at[1], p, scales), term + 1)

            @pl.when(more)
            def _(p=p):
                high_edge(0, later, p).start()

        for p in range(NP):
            high_ahead(turn, p).wait_recv()
            at = pl.ds(p * PIECE, PIECE)
            middle[0, at] = (fetched[turn, 0, at].astype(F32) + known[0, at]).astype(BF16)
        for p in range(NP):
            settle(0, pl.ds(p * PIECE, PIECE), top_piece(middle.at[0], p, scales), term + 1)

            @pl.when(more)
            def _(p=p):
                low_edge(0, later, p).start()

        return carry

    lax.fori_loop(1, ROUNDS, double, 0)
    for p in range(NP):
        low_ahead(ROUNDS % 2, p).wait_send()
        high_ahead(ROUNDS % 2, p).wait_send()
    last = 0

    lane = lax.broadcasted_iota(jnp.int32, (HALO, BS), 1)
    strip = jnp.zeros((HALO, BS), F32)
    for g in range(W):
        turned = pltpu.roll(ybuf[last, g * HALO : (g + 1) * HALO], (NB * (g + 1)) % BS, 1)
        strip = jnp.where(lane // NB == g, turned, strip)
    packed[...] = strip.astype(BF16)
    edge = pltpu.make_async_remote_copy(
        src_ref=packed,
        dst_ref=arrived,
        send_sem=edge_sem.at[0],
        recv_sem=edge_sem.at[1],
        device_id=(after, row),
        device_id_type=MESH,
    )
    edge.start()
    edge.wait()
    @pl.when(cut == 0)
    def _():
        arrived[...] = jnp.zeros((HALO, BS), BF16)

    def share(src, slots, sent, got, peers):
        copies = []
        for o, peer in enumerate(peers):
            copies.append(
                pltpu.make_async_remote_copy(
                    src_ref=src,
                    dst_ref=slots.at[o],
                    send_sem=sent.at[o],
                    recv_sem=got.at[o],
                    device_id=(cut, peer),
                    device_id_type=MESH,
                )
            )
            copies[-1].start()
        return copies

    def collect(copies, own, slots):
        summed = own
        for o, copy in enumerate(copies):
            copy.wait()
            summed = summed + slots[o]
        return summed

    boundary = arrived[...]
    square = tdot(boundary, boundary)
    eight = BS // W // W
    group = lax.broadcasted_iota(jnp.int32, (eight, BS), 1) // NB
    gram = jnp.zeros((NB, BS), F32)
    for g in range(W):
        rows = square[g * NB : (g + 1) * NB]
        gram = gram + (pltpu.roll(rows, (BS - NB * g) % BS, 1) if g else rows)
    tight = jnp.zeros((eight, BS), F32)
    for g in range(W):
        rows = gram[g * eight : (g + 1) * eight]
        tight = jnp.where(group == g, pltpu.roll(rows, NB * g, 1) if g else rows, tight)
    gpart[...] = tight
    gram_z = share(gpart, gzin, gzsend, gzrecv, zpeers)
    cross = jnp.zeros((NB, BS), F32)
    for g in range(W):
        mine = vbuf[last, pl.ds(g * HALO, HALO)]
        cross = cross + tdot(boundary, mine)[g * NB : (g + 1) * NB]
    cpart[...] = cross
    cross_z = share(cpart, czin, czsend, czrecv, zpeers)
    gmid[...] = collect(gram_z, tight, gzin)
    gram_x = share(gmid, gxin, gxsend, gxrecv, xpeers)
    cmid[...] = collect(cross_z, cross, czin)
    cross_x = share(cmid, cxin, cxsend, cxrecv, xpeers)
    tight = collect(gram_x, gmid[...], gxin)

    across = lax.broadcasted_iota(jnp.int32, (NB, BS), 1)
    down = lax.broadcasted_iota(jnp.int32, (NB, BS), 0)
    loose = [tight if g == 0 else pltpu.roll(tight, BS - NB * g, 1) for g in range(W)]
    whole = jnp.where(across < NB, jnp.concatenate(loose, axis=0), 0.0)
    whole = whole + jnp.where((across == down) | (across == down + NB), 1.0, 0.0)
    for j in range(NB):
        row_j = whole[j : j + 1] * (1.0 / whole[j : j + 1, j : j + 1])
        whole = jnp.where(down == j, row_j, whole - whole[:, j : j + 1] * row_j)
    summed = collect(cross_x, cmid[...], cxin)
    tall = jnp.concatenate(
        [jnp.zeros((NB, BS), F32), summed, jnp.zeros((2 * NB, BS), F32)], axis=0
    )
    right = jnp.dot(whole, tall, preferred_element_type=F32, precision=lax.Precision.HIGHEST)
    solved = right.astype(BF16).astype(F32)
    for g in range(W):
        above_rows = [jnp.zeros((NB, BS), F32)] * g
        below_rows = [jnp.zeros((NB, BS), F32)] * (W - 1 - g)
        spread = jnp.concatenate([*above_rows, solved, *below_rows], axis=0).astype(BF16)
        correction = dot(boundary, spread)
        rows = pl.ds(g * HALO, HALO)
        out[rows] = (ybuf[last, rows] - correction).astype(BF16)


def body(nz, nx, ncut, vectors, blocks, block_cols, counts, lower_end, upper_end, coeffs):
    blocks = blocks.reshape(RB * MAXB, BS, BS)
    hbm = pl.BlockSpec(memory_space=pltpu.HBM)
    stage = pltpu.VMEM((W * MAXB + 1, BS, BS), BF16)
    dma = pltpu.SemaphoreType.DMA
    return pl.pallas_call(
        functools.partial(kernel, nz, nx, ncut),
        out_shape=jax.ShapeDtypeStruct((OWN, BS), BF16),
        in_specs=[hbm] * 7,
        out_specs=pl.BlockSpec(memory_space=pltpu.VMEM),
        scratch_shapes=[
            pltpu.SMEM((MAXB, RB), jnp.int32),
            pltpu.SMEM((RB,), jnp.int32),
            pltpu.SMEM((1,), F32),
            pltpu.SMEM((1,), F32),
            pltpu.SMEM((1, DEG + 1), F32),
            stage,
            stage,
            stage,
            stage,
            pltpu.VMEM((QUADS, HALO, WIDE), BF16),
            pltpu.VMEM((2, OWN, BS), BF16),
            pltpu.VMEM((2, OWN, BS), F32),
            pltpu.VMEM((OWN, BS), F32),
            pltpu.VMEM((OWN, BS), BF16),
            pltpu.VMEM((HALO, BS), BF16),
            pltpu.VMEM((HALO, BS), BF16),
            pltpu.VMEM((2, HALO, BS), F32),
            pltpu.VMEM((2, 2, HALO, BS), BF16),
            pltpu.VMEM((2, HALO, BS), BF16),
            pltpu.VMEM((2, 2, HALO, BS), BF16),
            pltpu.VMEM((2, HALO, BS), F32),
            pltpu.VMEM((2, HALO, BS), BF16),
            pltpu.VMEM((2, HALO, HALO), BF16),
            pltpu.VMEM((8, BS), F32),
            pltpu.VMEM((nz - 1, 8, BS), F32),
            pltpu.VMEM((8, BS), F32),
            pltpu.VMEM((nx - 1, 8, BS), F32),
            pltpu.VMEM((NB, BS), F32),
            pltpu.VMEM((nz - 1, NB, BS), F32),
            pltpu.VMEM((NB, BS), F32),
            pltpu.VMEM((nx - 1, NB, BS), F32),
            dma((5,)),
            dma((QUADS,)),
            dma,
            *[dma((2, 2, NP))] * 4,
            dma((2, 2)),
            dma((2,)),
            *[dma((n,)) for n in 2 * [nz - 1, nz - 1, nx - 1, nx - 1]],
        ],
        compiler_params=pltpu.CompilerParams(
            collective_id=0, has_side_effects=True, vmem_limit_bytes=60 * 1024 * 1024
        ),
    )(vectors, blocks, block_cols.T, counts, lower_end, upper_end, coeffs)


def solution(mesh):
    rows = mesh.shape["rows"]
    nx = 4 if rows == 32 else 2
    return jax.shard_map(
        functools.partial(body, rows // nx, nx, mesh.shape["cuts"]),
        mesh=mesh,
        in_specs=(
            P("rows", "cuts"),
            P("rows", None, None, None),
            P("rows", None),
            P("rows"),
            P("cuts"),
            P("cuts"),
            P("cuts", None),
        ),
        out_specs=P("rows", "cuts"),
        check_vma=False,
    )
```

```python
import functools

import jax
import jax.numpy as jnp
from jax import lax
from jax.experimental import pallas as pl
from jax.experimental.pallas import tpu as pltpu
from jax.sharding import PartitionSpec as P

BS = 128
MAXB = 8
W = 4
DEG = 6
PASSES = 2
NB = 32
RB = 16
HALO = W * BS
NP = 2
PIECE = HALO // NP
ROUNDS = PASSES * DEG // 2
OWN = RB * BS
QUADS = RB // W
WIDE = 3 * W * BS
MESH = pl.DeviceIdType.MESH
F32 = jnp.float32
BF16 = jnp.bfloat16


def dot(a, b):
    return jnp.dot(a, b, preferred_element_type=F32)


def tdot(a, b):
    return lax.dot_general(a, b, (((0,), (0,)), ((), ())), preferred_element_type=F32)


def kernel(
    nz,
    nx,
    ncut,
    vec,
    blocks,
    cols_in,
    counts_in,
    lower_in,
    upper_in,
    coeffs_in,
    out,
    cols,
    counts,
    lower,
    upper,
    coeffs,
    stage0,
    stage1,
    stage2,
    stage3,
    dense,
    vbuf,
    ybuf,
    total,
    start,
    packed,
    arrived,
    acc,
    halo,
    ahead,
    fetched,
    known,
    early,
    middle,
    corner,
    gpart,
    gzin,
    gmid,
    gxin,
    cpart,
    czin,
    cmid,
    cxin,
    small_sem,
    block_sem,
    vec_sem,
    send_sem,
    recv_sem,
    asend,
    arecv,
    csend,
    crecv,
    wsend,
    wrecv,
    edge_sem,
    gzsend,
    gzrecv,
    gxsend,
    gxrecv,
    czsend,
    czrecv,
    cxsend,
    cxrecv,
):
    stages = (stage0, stage1, stage2, stage3)
    row = lax.axis_index("rows")
    cut = lax.axis_index("cuts")
    nrow = nz * nx
    z = lax.rem(row, nz)
    x = lax.div(row, nz)
    low = lax.rem(row + nrow - 1, nrow)
    high = lax.rem(row + 1, nrow)
    after = lax.rem(cut + 1, ncut)
    before = lax.rem(cut + ncut - 1, ncut)
    zpeers = [x * nz + lax.rem(z + o, nz) for o in range(1, nz)]
    xpeers = [lax.rem(x + o, nx) * nz + z for o in range(1, nx)]

    vec_copy = pltpu.make_async_copy(vec, start, vec_sem)
    vec_copy.start()
    small = []
    for n, (src, dst) in enumerate(
        ((lower_in, lower), (upper_in, upper), (coeffs_in, coeffs), (cols_in, cols), (counts_in, counts))
    ):
        small.append(pltpu.make_async_copy(src, dst, small_sem.at[n]))
        small[-1].start()
    block_copies = []
    for q in range(QUADS):
        copy = pltpu.make_async_copy(
            blocks.at[pl.ds(q * W * MAXB, W * MAXB)],
            stages[q].at[pl.ds(0, W * MAXB)],
            block_sem.at[q],
        )
        copy.start()
        block_copies.append(copy)

    corner[...] = jnp.zeros((2, HALO, HALO), BF16)
    barrier = pltpu.get_barrier_semaphore()
    greeted = 0
    for other in [low, high, *zpeers, *xpeers]:
        pl.semaphore_signal(barrier, inc=1, device_id=(cut, other), device_id_type=MESH)
        greeted += 1
    for other in (before, after):
        pl.semaphore_signal(barrier, inc=1, device_id=(other, row), device_id_type=MESH)
        greeted += 1

    for q in range(QUADS):
        dense[q] = jnp.zeros((W * BS, WIDE), BF16)
        stages[q][W * MAXB] = jnp.zeros((BS, BS), BF16)
    for copy in small:
        copy.wait()
    centre = (lower[0] + upper[0]) * 0.5
    half = (upper[0] - lower[0]) * 0.5
    inverse = 1.0 / half

    pl.semaphore_wait(barrier, greeted)

    def side_copy(src, dst, sent, got, device):
        return pltpu.make_async_remote_copy(
            src_ref=src,
            dst_ref=dst,
            send_sem=sent,
            recv_sem=got,
            device_id=(cut, device),
            device_id_type=MESH,
        )

    def to_low(src, turn, p):
        return side_copy(
            src,
            halo.at[turn, 1, pl.ds(p * PIECE, PIECE)],
            send_sem.at[0, turn, p],
            recv_sem.at[1, turn, p],
            low,
        )

    def to_high(src, turn, p):
        return side_copy(
            src,
            halo.at[turn, 0, pl.ds(p * PIECE, PIECE)],
            send_sem.at[1, turn, p],
            recv_sem.at[0, turn, p],
            high,
        )

    def low_edge(slot, turn, p):
        return to_low(vbuf.at[slot, pl.ds(p * PIECE, PIECE)], turn, p)

    def high_edge(slot, turn, p):
        return to_high(vbuf.at[slot, pl.ds(OWN - HALO + p * PIECE, PIECE)], turn, p)

    def low_ahead(turn, p):
        at = pl.ds(p * PIECE, PIECE)
        return side_copy(
            ahead.at[0, at],
            fetched.at[turn, 1, at],
            asend.at[0, turn, p],
            arecv.at[1, turn, p],
            low,
        )

    def high_ahead(turn, p):
        at = pl.ds(p * PIECE, PIECE)
        return side_copy(
            ahead.at[1, at],
            fetched.at[turn, 0, at],
            asend.at[1, turn, p],
            arecv.at[0, turn, p],
            high,
        )

    def low_corner(i):
        at, lanes = pl.ds(i * BS, BS), pl.ds(i * BS, (W - i) * BS)
        return side_copy(
            dense.at[0, at, lanes], corner.at[1, at, lanes], csend.at[0, i], crecv.at[1, i], low
        )

    def high_corner(i):
        at, lanes = pl.ds(i * BS, BS), pl.ds(0, (i + 1) * BS)
        return side_copy(
            dense.at[QUADS - 1, at, pl.ds(2 * HALO, (i + 1) * BS)],
            corner.at[0, at, lanes],
            csend.at[1, i],
            crecv.at[0, i],
            high,
        )

    def swapped(side, i):
        at = pl.ds(i * BS, BS)
        lanes = pl.ds(i * BS, (W - i) * BS) if side else pl.ds(0, (i + 1) * BS)
        return pltpu.make_async_remote_copy(
            src_ref=corner.at[side, at, lanes],
            dst_ref=corner.at[side, at, lanes],
            send_sem=wsend.at[side, i],
            recv_sem=wrecv.at[side, i],
            device_id=(cut + 1 - 2 * lax.rem(cut, 2), row),
            device_id_type=MESH,
        )

    halves = ((0, (0, W - 1)), (1, (1, W - 2)))

    for p in range(NP):
        to_high(vec.at[pl.ds(OWN - HALO + p * PIECE, PIECE)], 0, p).start()
        to_low(vec.at[pl.ds(p * PIECE, PIECE)], 0, p).start()

    vec_copy.wait()
    vbuf[0] = start[...]
    first = start[...].astype(F32)
    ybuf[0] = first
    ybuf[1] = jnp.zeros((OWN, BS), F32)
    total[...] = coeffs[0, 0] * first

    for q in range(QUADS):
        block_copies[q].wait()

        def place(i, carry, q=q):
            r = q * W + i
            base = row * RB + r - W
            live = counts[r]
            near = [jnp.where(s < live, cols[s, r] - base, -1) for s in range(MAXB)]
            for d in range(2 * W + 1):
                slot = jnp.int32(W * MAXB)
                for s in range(MAXB):
                    slot = jnp.where(near[s] == d, i * MAXB + s, slot)
                rows = pl.ds(pl.multiple_of(i * BS, BS), BS)
                lanes = pl.ds(pl.multiple_of((i + d) * BS, BS), BS)
                dense[q, rows, lanes] = stages[q][slot]
            return carry

        lax.fori_loop(0, W, place, 0)

    def factors(term):
        opening = term == 0
        scale = jnp.where(opening, 1.0, 2.0) * inverse
        return scale, scale * centre, jnp.where(opening, 0.0, 1.0)

    def recur(now, new, rows, product, scales):
        scale, shift, keep = scales
        return scale * product - shift * ybuf[now, rows] - keep * ybuf[new, rows]

    def settle(new, rows, upcoming, term):
        closing = term == DEG - 1
        summed = total[rows] + coeffs[0, term + 1] * upcoming
        value = jnp.where(closing, summed, upcoming)
        total[rows] = jnp.where(closing, coeffs[0, 0] * summed, summed)
        ybuf[new, rows] = value
        vbuf[new, rows] = value.astype(BF16)

    def inner(now, new, term, scales):
        pair = 2 * BS
        wide = (2 * W + 2) * BS
        for q in (1, 2):
            for j in (0, 1):
                at = q * HALO + j * pair
                product = dot(
                    dense[q, j * pair : (j + 1) * pair, j * pair : j * pair + wide],
                    vbuf[now, pl.ds(at - HALO, wide)],
                )
                rows = pl.ds(at, pair)
                settle(new, rows, recur(now, new, rows, product, scales), term)

    top, bottom = pl.ds(0, HALO), pl.ds(OWN - HALO, HALO)

    def own_part(now, new, scales):
        product = dot(dense[QUADS - 1, :, : 2 * HALO], vbuf[now, pl.ds(OWN - 2 * HALO, 2 * HALO)])
        acc[1] = recur(now, new, bottom, product, scales)
        product = dot(dense[0, :, HALO:], vbuf[now, pl.ds(0, 2 * HALO)])
        acc[0] = recur(now, new, top, product, scales)

    def bottom_piece(src, p, scales):
        inside = slice(p * PIECE, (p + 1) * PIECE)
        deep = (p + 1) * PIECE
        product = dot(dense[QUADS - 1, inside, 2 * HALO : 2 * HALO + deep], src[pl.ds(0, deep)])
        return acc[1, inside] + scales[0] * product

    def top_piece(src, p, scales):
        inside = slice(p * PIECE, (p + 1) * PIECE)
        product = dot(
            dense[0, inside, p * PIECE : HALO], src[pl.ds(p * PIECE, HALO - p * PIECE)]
        )
        return acc[0, inside] + scales[0] * product

    def edges(new, turn):
        return [f(new, turn, p) for f in (high_edge, low_edge) for p in range(NP)]

    def step(k, carry):
        now = lax.rem(k, 2)
        new = 1 - now
        scales = factors(k)
        own_part(now, new, scales)
        inner(now, new, k, scales)

        @pl.when(k > 0)
        def _():
            for copy in edges(new, new):
                copy.wait_send()

        for p in range(NP):
            low_edge(now, now, p).wait_recv()
            settle(
                new,
                pl.ds(OWN - HALO + p * PIECE, PIECE),
                bottom_piece(halo.at[now, 1], p, scales),
                k,
            )
            high_edge(new, new, p).start()
        for p in range(NP):
            high_edge(now, now, p).wait_recv()
        for p in range(NP):
            settle(new, pl.ds(p * PIECE, PIECE), top_piece(halo.at[now, 0], p, scales), k)
            low_edge(new, new, p).start()
        return carry

    lax.fori_loop(0, 1, step, 0)
    for parity, mine in halves:

        @pl.when(lax.rem(cut, 2) == parity)
        def _(mine=mine):
            for i in mine:
                high_corner(i).start()
                low_corner(i).start()

    lax.fori_loop(1, 2, step, 0)
    for parity, mine in halves:

        @pl.when(lax.rem(cut, 2) == parity)
        def _(mine=mine):
            for i in mine:
                for copy in (high_corner(i), low_corner(i)):
                    copy.wait()
                for side in (0, 1):
                    swapped(side, i).start()

    for copy in edges(1, 1):
        copy.wait_send()

    def double(j, carry):
        turn = lax.rem(j + 1, 2)
        later = 1 - turn
        term = lax.rem(2 * j, DEG)
        scales = factors(term)

        @pl.when(j > 1)
        def _():
            for p in range(NP):
                low_ahead(later, p).wait_send()
                high_ahead(later, p).wait_send()

        own_part(0, 1, scales)
        ahead[1] = acc[1].astype(BF16)
        for p in range(NP):
            high_ahead(turn, p).start()
        ahead[0] = acc[0].astype(BF16)
        for p in range(NP):
            low_ahead(turn, p).start()
        inner(0, 1, term, scales)
        early[1] = dot(dense[QUADS - 1, :, :HALO], vbuf[1, pl.ds(OWN - 2 * HALO, HALO)])
        early[0] = dot(dense[0, :, 2 * HALO :], vbuf[1, pl.ds(HALO, HALO)])

        @pl.when(j == 1)
        def _():
            for parity, mine in halves:
                other = halves[1 - parity][1]

                @pl.when(lax.rem(cut, 2) == parity)
                def _(mine=mine, other=other):
                    for side in (0, 1):
                        for i in mine:
                            swapped(side, i).wait_send()
                        for i in other:
                            swapped(side, i).wait_recv()

        known[1] = scales[0] * dot(corner[1], vbuf[0, bottom])
        known[0] = scales[0] * dot(corner[0], vbuf[0, top])
        for p in range(NP):
            low_edge(0, turn, p).wait_recv()
        product = dot(dense[QUADS - 1, :, 2 * HALO :], halo[turn, 1])
        settle(1, bottom, acc[1] + scales[0] * product, term)
        scales = factors(term + 1)
        product = early[1] + dot(dense[QUADS - 1, :, HALO : 2 * HALO], vbuf[1, bottom])
        acc[1] = recur(1, 0, bottom, product, scales)
        for p in range(NP):
            high_edge(0, turn, p).wait_recv()
        product = dot(dense[0, :, :HALO], halo[turn, 0])
        settle(1, top, acc[0] + factors(term)[0] * product, term)
        product = early[0] + dot(dense[0, :, HALO : 2 * HALO], vbuf[1, top])
        acc[0] = recur(1, 0, top, product, scales)
        for copy in edges(0, turn):
            copy.wait_send()
        more = j < ROUNDS - 1

        @pl.when(jnp.logical_not(more))
        def _():
            inner(1, 0, term + 1, scales)

        for p in range(NP):
            low_ahead(turn, p).wait_recv()
            at = pl.ds(p * PIECE, PIECE)
            middle[1, at] = (fetched[turn, 1, at].astype(F32) + known[1, at]).astype(BF16)
            rows = pl.ds(OWN - HALO + p * PIECE, PIECE)
            settle(0, rows, bottom_piece(middle.at[1], p, scales), term + 1)

            @pl.when(more)
            def _(p=p):
                high_edge(0, later, p).start()

        for p in range(NP):
            high_ahead(turn, p).wait_recv()
            at = pl.ds(p * PIECE, PIECE)
            middle[0, at] = (fetched[turn, 0, at].astype(F32) + known[0, at]).astype(BF16)
        for p in range(NP):
            settle(0, pl.ds(p * PIECE, PIECE), top_piece(middle.at[0], p, scales), term + 1)

            @pl.when(more)
            def _(p=p):
                low_edge(0, later, p).start()

        @pl.when(more)
        def _():
            inner(1, 0, term + 1, scales)

        return carry

    lax.fori_loop(1, ROUNDS, double, 0)
    for p in range(NP):
        low_ahead(ROUNDS % 2, p).wait_send()
        high_ahead(ROUNDS % 2, p).wait_send()
    last = 0

    lane = lax.broadcasted_iota(jnp.int32, (HALO, BS), 1)
    strip = jnp.zeros((HALO, BS), F32)
    for g in range(W):
        turned = pltpu.roll(ybuf[last, g * HALO : (g + 1) * HALO], (NB * (g + 1)) % BS, 1)
        strip = jnp.where(lane // NB == g, turned, strip)
    packed[...] = strip.astype(BF16)
    edge = pltpu.make_async_remote_copy(
        src_ref=packed,
        dst_ref=arrived,
        send_sem=edge_sem.at[0],
        recv_sem=edge_sem.at[1],
        device_id=(after, row),
        device_id_type=MESH,
    )
    edge.start()
    edge.wait()
    @pl.when(cut == 0)
    def _():
        arrived[...] = jnp.zeros((HALO, BS), BF16)

    def share(src, slots, sent, got, peers):
        copies = []
        for o, peer in enumerate(peers):
            copies.append(
                pltpu.make_async_remote_copy(
                    src_ref=src,
                    dst_ref=slots.at[o],
                    send_sem=sent.at[o],
                    recv_sem=got.at[o],
                    device_id=(cut, peer),
                    device_id_type=MESH,
                )
            )
            copies[-1].start()
        return copies

    def collect(copies, own, slots):
        summed = own
        for o, copy in enumerate(copies):
            copy.wait()
            summed = summed + slots[o]
        return summed

    boundary = arrived[...]
    square = tdot(boundary, boundary)
    eight = BS // W // W
    group = lax.broadcasted_iota(jnp.int32, (eight, BS), 1) // NB
    gram = jnp.zeros((NB, BS), F32)
    for g in range(W):
        rows = square[g * NB : (g + 1) * NB]
        gram = gram + (pltpu.roll(rows, (BS - NB * g) % BS, 1) if g else rows)
    tight = jnp.zeros((eight, BS), F32)
    for g in range(W):
        rows = gram[g * eight : (g + 1) * eight]
        tight = jnp.where(group == g, pltpu.roll(rows, NB * g, 1) if g else rows, tight)
    gpart[...] = tight
    gram_z = share(gpart, gzin, gzsend, gzrecv, zpeers)
    cross = jnp.zeros((NB, BS), F32)
    for g in range(W):
        mine = vbuf[last, pl.ds(g * HALO, HALO)]
        cross = cross + tdot(boundary, mine)[g * NB : (g + 1) * NB]
    cpart[...] = cross
    cross_z = share(cpart, czin, czsend, czrecv, zpeers)
    gmid[...] = collect(gram_z, tight, gzin)
    gram_x = share(gmid, gxin, gxsend, gxrecv, xpeers)
    cmid[...] = collect(cross_z, cross, czin)
    cross_x = share(cmid, cxin, cxsend, cxrecv, xpeers)
    tight = collect(gram_x, gmid[...], gxin)

    across = lax.broadcasted_iota(jnp.int32, (NB, BS), 1)
    down = lax.broadcasted_iota(jnp.int32, (NB, BS), 0)
    loose = [tight if g == 0 else pltpu.roll(tight, BS - NB * g, 1) for g in range(W)]
    whole = jnp.where(across < NB, jnp.concatenate(loose, axis=0), 0.0)
    whole = whole + jnp.where((across == down) | (across == down + NB), 1.0, 0.0)
    for j in range(NB):
        row_j = whole[j : j + 1] * (1.0 / whole[j : j + 1, j : j + 1])
        whole = jnp.where(down == j, row_j, whole - whole[:, j : j + 1] * row_j)
    summed = collect(cross_x, cmid[...], cxin)
    tall = jnp.concatenate(
        [jnp.zeros((NB, BS), F32), summed, jnp.zeros((2 * NB, BS), F32)], axis=0
    )
    right = jnp.dot(whole, tall, preferred_element_type=F32, precision=lax.Precision.HIGHEST)
    solved = right.astype(BF16).astype(F32)
    for g in range(W):
        above_rows = [jnp.zeros((NB, BS), F32)] * g
        below_rows = [jnp.zeros((NB, BS), F32)] * (W - 1 - g)
        spread = jnp.concatenate([*above_rows, solved, *below_rows], axis=0).astype(BF16)
        correction = dot(boundary, spread)
        rows = pl.ds(g * HALO, HALO)
        out[rows] = (ybuf[last, rows] - correction).astype(BF16)


def body(nz, nx, ncut, vectors, blocks, block_cols, counts, lower_end, upper_end, coeffs):
    blocks = blocks.reshape(RB * MAXB, BS, BS)
    hbm = pl.BlockSpec(memory_space=pltpu.HBM)
    stage = pltpu.VMEM((W * MAXB + 1, BS, BS), BF16)
    dma = pltpu.SemaphoreType.DMA
    return pl.pallas_call(
        functools.partial(kernel, nz, nx, ncut),
        out_shape=jax.ShapeDtypeStruct((OWN, BS), BF16),
        in_specs=[hbm] * 7,
        out_specs=pl.BlockSpec(memory_space=pltpu.VMEM),
        scratch_shapes=[
            pltpu.SMEM((MAXB, RB), jnp.int32),
            pltpu.SMEM((RB,), jnp.int32),
            pltpu.SMEM((1,), F32),
            pltpu.SMEM((1,), F32),
            pltpu.SMEM((1, DEG + 1), F32),
            stage,
            stage,
            stage,
            stage,
            pltpu.VMEM((QUADS, HALO, WIDE), BF16),
            pltpu.VMEM((2, OWN, BS), BF16),
            pltpu.VMEM((2, OWN, BS), F32),
            pltpu.VMEM((OWN, BS), F32),
            pltpu.VMEM((OWN, BS), BF16),
            pltpu.VMEM((HALO, BS), BF16),
            pltpu.VMEM((HALO, BS), BF16),
            pltpu.VMEM((2, HALO, BS), F32),
            pltpu.VMEM((2, 2, HALO, BS), BF16),
            pltpu.VMEM((2, HALO, BS), BF16),
            pltpu.VMEM((2, 2, HALO, BS), BF16),
            pltpu.VMEM((2, HALO, BS), F32),
            pltpu.VMEM((2, HALO, BS), F32),
            pltpu.VMEM((2, HALO, BS), BF16),
            pltpu.VMEM((2, HALO, HALO), BF16),
            pltpu.VMEM((8, BS), F32),
            pltpu.VMEM((nz - 1, 8, BS), F32),
            pltpu.VMEM((8, BS), F32),
            pltpu.VMEM((nx - 1, 8, BS), F32),
            pltpu.VMEM((NB, BS), F32),
            pltpu.VMEM((nz - 1, NB, BS), F32),
            pltpu.VMEM((NB, BS), F32),
            pltpu.VMEM((nx - 1, NB, BS), F32),
            dma((5,)),
            dma((QUADS,)),
            dma,
            *[dma((2, 2, NP))] * 4,
            *[dma((2, W))] * 4,
            dma((2,)),
            *[dma((n,)) for n in 2 * [nz - 1, nz - 1, nx - 1, nx - 1]],
        ],
        compiler_params=pltpu.CompilerParams(
            collective_id=0, has_side_effects=True, vmem_limit_bytes=60 * 1024 * 1024
        ),
    )(vectors, blocks, block_cols.T, counts, lower_end, upper_end, coeffs)


def solution(mesh):
    rows = mesh.shape["rows"]
    nx = 4 if rows == 32 else 2
    return jax.shard_map(
        functools.partial(body, rows // nx, nx, mesh.shape["cuts"]),
        mesh=mesh,
        in_specs=(
            P("rows", "cuts"),
            P("rows", None, None, None),
            P("rows", None),
            P("rows"),
            P("cuts"),
            P("cuts"),
            P("cuts", None),
        ),
        out_specs=P("rows", "cuts"),
        check_vma=False,
    )
```

```python
import functools

import jax
import jax.numpy as jnp
from jax import lax
from jax.experimental import pallas as pl
from jax.experimental.pallas import tpu as pltpu
from jax.sharding import PartitionSpec as P

BS = 128
MAXB = 8
W = 4
DEG = 6
PASSES = 2
NB = 32
RB = 16
HALO = W * BS
NP = 2
PIECE = HALO // NP
ROUNDS = PASSES * DEG // 2
OWN = RB * BS
QUADS = RB // W
WIDE = 3 * W * BS
MESH = pl.DeviceIdType.MESH
F32 = jnp.float32
BF16 = jnp.bfloat16


def dot(a, b):
    return jnp.dot(a, b, preferred_element_type=F32)


def tdot(a, b):
    return lax.dot_general(a, b, (((0,), (0,)), ((), ())), preferred_element_type=F32)


def kernel(
    nz,
    nx,
    ncut,
    vec,
    blocks,
    cols_in,
    counts_in,
    lower_in,
    upper_in,
    coeffs_in,
    out,
    cols,
    counts,
    lower,
    upper,
    coeffs,
    stage0,
    stage1,
    stage2,
    stage3,
    dense,
    vbuf,
    ybuf,
    total,
    start,
    packed,
    arrived,
    acc,
    halo,
    ahead,
    fetched,
    known,
    early,
    middle,
    corner,
    gpart,
    gzin,
    gmid,
    gxin,
    cpart,
    czin,
    cmid,
    cxin,
    small_sem,
    block_sem,
    vec_sem,
    send_sem,
    recv_sem,
    asend,
    arecv,
    csend,
    crecv,
    wsend,
    wrecv,
    edge_sem,
    gzsend,
    gzrecv,
    gxsend,
    gxrecv,
    czsend,
    czrecv,
    cxsend,
    cxrecv,
):
    stages = (stage0, stage1, stage2, stage3)
    row = lax.axis_index("rows")
    cut = lax.axis_index("cuts")
    nrow = nz * nx
    z = lax.rem(row, nz)
    x = lax.div(row, nz)
    low = lax.rem(row + nrow - 1, nrow)
    high = lax.rem(row + 1, nrow)
    after = lax.rem(cut + 1, ncut)
    before = lax.rem(cut + ncut - 1, ncut)
    zpeers = [x * nz + lax.rem(z + o, nz) for o in range(1, nz)]
    xpeers = [lax.rem(x + o, nx) * nz + z for o in range(1, nx)]

    vec_copy = pltpu.make_async_copy(vec, start, vec_sem)
    vec_copy.start()
    small = []
    for n, (src, dst) in enumerate(
        ((lower_in, lower), (upper_in, upper), (coeffs_in, coeffs), (cols_in, cols), (counts_in, counts))
    ):
        small.append(pltpu.make_async_copy(src, dst, small_sem.at[n]))
        small[-1].start()
    block_copies = []
    for q in range(QUADS):
        copy = pltpu.make_async_copy(
            blocks.at[pl.ds(q * W * MAXB, W * MAXB)],
            stages[q].at[pl.ds(0, W * MAXB)],
            block_sem.at[q],
        )
        copy.start()
        block_copies.append(copy)

    corner[...] = jnp.zeros((2, HALO, HALO), BF16)
    barrier = pltpu.get_barrier_semaphore()
    greeted = 0
    for other in [low, high, *zpeers, *xpeers]:
        pl.semaphore_signal(barrier, inc=1, device_id=(cut, other), device_id_type=MESH)
        greeted += 1
    for other in (before, after):
        pl.semaphore_signal(barrier, inc=1, device_id=(other, row), device_id_type=MESH)
        greeted += 1

    for q in range(QUADS):
        dense[q] = jnp.zeros((W * BS, WIDE), BF16)
        stages[q][W * MAXB] = jnp.zeros((BS, BS), BF16)
    for copy in small:
        copy.wait()
    centre = (lower[0] + upper[0]) * 0.5
    half = (upper[0] - lower[0]) * 0.5
    inverse = 1.0 / half

    pl.semaphore_wait(barrier, greeted)

    def side_copy(src, dst, sent, got, device):
        return pltpu.make_async_remote_copy(
            src_ref=src,
            dst_ref=dst,
            send_sem=sent,
            recv_sem=got,
            device_id=(cut, device),
            device_id_type=MESH,
        )

    def to_low(src, turn, p):
        return side_copy(
            src,
            halo.at[turn, 1, pl.ds(p * PIECE, PIECE)],
            send_sem.at[0, turn, p],
            recv_sem.at[1, turn, p],
            low,
        )

    def to_high(src, turn, p):
        return side_copy(
            src,
            halo.at[turn, 0, pl.ds(p * PIECE, PIECE)],
            send_sem.at[1, turn, p],
            recv_sem.at[0, turn, p],
            high,
        )

    def low_edge(slot, turn, p):
        return to_low(vbuf.at[slot, pl.ds(p * PIECE, PIECE)], turn, p)

    def high_edge(slot, turn, p):
        return to_high(vbuf.at[slot, pl.ds(OWN - HALO + p * PIECE, PIECE)], turn, p)

    def low_ahead(turn, p):
        at = pl.ds(p * PIECE, PIECE)
        return side_copy(
            ahead.at[0, at],
            fetched.at[turn, 1, at],
            asend.at[0, turn, p],
            arecv.at[1, turn, p],
            low,
        )

    def high_ahead(turn, p):
        at = pl.ds(p * PIECE, PIECE)
        return side_copy(
            ahead.at[1, at],
            fetched.at[turn, 0, at],
            asend.at[1, turn, p],
            arecv.at[0, turn, p],
            high,
        )

    def low_corner(i):
        at, lanes = pl.ds(i * BS, BS), pl.ds(i * BS, (W - i) * BS)
        return side_copy(
            dense.at[0, at, lanes], corner.at[1, at, lanes], csend.at[0, i], crecv.at[1, i], low
        )

    def high_corner(i):
        at, lanes = pl.ds(i * BS, BS), pl.ds(0, (i + 1) * BS)
        return side_copy(
            dense.at[QUADS - 1, at, pl.ds(2 * HALO, (i + 1) * BS)],
            corner.at[0, at, lanes],
            csend.at[1, i],
            crecv.at[0, i],
            high,
        )

    def swapped(side, i):
        at = pl.ds(i * BS, BS)
        lanes = pl.ds(i * BS, (W - i) * BS) if side else pl.ds(0, (i + 1) * BS)
        return pltpu.make_async_remote_copy(
            src_ref=corner.at[side, at, lanes],
            dst_ref=corner.at[side, at, lanes],
            send_sem=wsend.at[side, i],
            recv_sem=wrecv.at[side, i],
            device_id=(cut + 1 - 2 * lax.rem(cut, 2), row),
            device_id_type=MESH,
        )

    halves = ((0, (0, W - 1)), (1, (1, W - 2)))

    for p in range(NP):
        to_high(vec.at[pl.ds(OWN - HALO + p * PIECE, PIECE)], 0, p).start()
        to_low(vec.at[pl.ds(p * PIECE, PIECE)], 0, p).start()

    vec_copy.wait()
    vbuf[0] = start[...]
    first = start[...].astype(F32)
    ybuf[0] = first
    ybuf[1] = jnp.zeros((OWN, BS), F32)
    total[...] = coeffs[0, 0] * first

    for q in range(QUADS):
        block_copies[q].wait()

        def place(i, carry, q=q):
            r = q * W + i
            base = row * RB + r - W
            live = counts[r]
            near = [jnp.where(s < live, cols[s, r] - base, -1) for s in range(MAXB)]
            for d in range(2 * W + 1):
                slot = jnp.int32(W * MAXB)
                for s in range(MAXB):
                    slot = jnp.where(near[s] == d, i * MAXB + s, slot)
                rows = pl.ds(pl.multiple_of(i * BS, BS), BS)
                lanes = pl.ds(pl.multiple_of((i + d) * BS, BS), BS)
                dense[q, rows, lanes] = stages[q][slot]
            return carry

        lax.fori_loop(0, W, place, 0)

    def factors(term):
        opening = term == 0
        scale = jnp.where(opening, 1.0, 2.0) * inverse
        return scale, scale * centre, jnp.where(opening, 0.0, 1.0)

    def recur(now, new, rows, product, scales):
        scale, shift, keep = scales
        return scale * product - shift * ybuf[now, rows] - keep * ybuf[new, rows]

    def settle(new, rows, upcoming, term):
        closing = term == DEG - 1
        summed = total[rows] + coeffs[0, term + 1] * upcoming
        value = jnp.where(closing, summed, upcoming)
        total[rows] = jnp.where(closing, coeffs[0, 0] * summed, summed)
        ybuf[new, rows] = value
        vbuf[new, rows] = value.astype(BF16)

    def inner(now, new, term, scales):
        pair = 2 * BS
        wide = (2 * W + 2) * BS
        for q in (1, 2):
            for j in (0, 1):
                at = q * HALO + j * pair
                product = dot(
                    dense[q, j * pair : (j + 1) * pair, j * pair : j * pair + wide],
                    vbuf[now, pl.ds(at - HALO, wide)],
                )
                rows = pl.ds(at, pair)
                settle(new, rows, recur(now, new, rows, product, scales), term)

    top, bottom = pl.ds(0, HALO), pl.ds(OWN - HALO, HALO)

    def own_part(now, new, scales):
        product = dot(dense[QUADS - 1, :, : 2 * HALO], vbuf[now, pl.ds(OWN - 2 * HALO, 2 * HALO)])
        acc[1] = recur(now, new, bottom, product, scales)
        product = dot(dense[0, :, HALO:], vbuf[now, pl.ds(0, 2 * HALO)])
        acc[0] = recur(now, new, top, product, scales)

    def bottom_piece(src, p, scales):
        inside = slice(p * PIECE, (p + 1) * PIECE)
        deep = (p + 1) * PIECE
        product = dot(dense[QUADS - 1, inside, 2 * HALO : 2 * HALO + deep], src[pl.ds(0, deep)])
        return acc[1, inside] + scales[0] * product

    def top_piece(src, p, scales):
        inside = slice(p * PIECE, (p + 1) * PIECE)
        product = dot(
            dense[0, inside, p * PIECE : HALO], src[pl.ds(p * PIECE, HALO - p * PIECE)]
        )
        return acc[0, inside] + scales[0] * product

    def edges(new, turn):
        return [f(new, turn, p) for f in (high_edge, low_edge) for p in range(NP)]

    def step(k, carry):
        now = lax.rem(k, 2)
        new = 1 - now
        scales = factors(k)
        own_part(now, new, scales)
        inner(now, new, k, scales)

        @pl.when(k > 0)
        def _():
            for copy in edges(new, new):
                copy.wait_send()

        for p in range(NP):
            low_edge(now, now, p).wait_recv()
            settle(
                new,
                pl.ds(OWN - HALO + p * PIECE, PIECE),
                bottom_piece(halo.at[now, 1], p, scales),
                k,
            )
            high_edge(new, new, p).start()
        for p in range(NP):
            high_edge(now, now, p).wait_recv()
        for p in range(NP):
            settle(new, pl.ds(p * PIECE, PIECE), top_piece(halo.at[now, 0], p, scales), k)
            low_edge(new, new, p).start()
        return carry

    lax.fori_loop(0, 1, step, 0)
    for parity, mine in halves:

        @pl.when(lax.rem(cut, 2) == parity)
        def _(mine=mine):
            for i in mine:
                high_corner(i).start()
                low_corner(i).start()

    lax.fori_loop(1, 2, step, 0)
    for parity, mine in halves:

        @pl.when(lax.rem(cut, 2) == parity)
        def _(mine=mine):
            for i in mine:
                for copy in (high_corner(i), low_corner(i)):
                    copy.wait()
                for side in (0, 1):
                    swapped(side, i).start()

    for copy in edges(1, 1):
        copy.wait_send()

    def double(j, carry):
        turn = lax.rem(j + 1, 2)
        later = 1 - turn
        term = lax.rem(2 * j, DEG)
        scales = factors(term)

        @pl.when(j > 1)
        def _():
            for p in range(NP):
                low_ahead(later, p).wait_send()
                high_ahead(later, p).wait_send()

        own_part(0, 1, scales)
        ahead[1] = acc[1].astype(BF16)
        for p in range(NP):
            high_ahead(turn, p).start()
        ahead[0] = acc[0].astype(BF16)
        for p in range(NP):
            low_ahead(turn, p).start()
        inner(0, 1, term, scales)
        early[1] = dot(dense[QUADS - 1, :, :HALO], vbuf[1, pl.ds(OWN - 2 * HALO, HALO)])
        early[0] = dot(dense[0, :, 2 * HALO :], vbuf[1, pl.ds(HALO, HALO)])

        @pl.when(j == 1)
        def _():
            for parity, mine in halves:
                other = halves[1 - parity][1]

                @pl.when(lax.rem(cut, 2) == parity)
                def _(mine=mine, other=other):
                    for side in (0, 1):
                        for i in mine:
                            swapped(side, i).wait_send()
                        for i in other:
                            swapped(side, i).wait_recv()

        known[1] = scales[0] * dot(corner[1], vbuf[0, bottom])
        known[0] = scales[0] * dot(corner[0], vbuf[0, top])
        for p in range(NP):
            low_edge(0, turn, p).wait_recv()
        product = dot(dense[QUADS - 1, :, 2 * HALO :], halo[turn, 1])
        settle(1, bottom, acc[1] + scales[0] * product, term)
        scales = factors(term + 1)
        product = early[1] + dot(dense[QUADS - 1, :, HALO : 2 * HALO], vbuf[1, bottom])
        acc[1] = recur(1, 0, bottom, product, scales)
        for p in range(NP):
            high_edge(0, turn, p).wait_recv()
        product = dot(dense[0, :, :HALO], halo[turn, 0])
        settle(1, top, acc[0] + factors(term)[0] * product, term)
        product = early[0] + dot(dense[0, :, HALO : 2 * HALO], vbuf[1, top])
        acc[0] = recur(1, 0, top, product, scales)
        for copy in edges(0, turn):
            copy.wait_send()
        more = j < ROUNDS - 1

        inner(1, 0, term + 1, scales)
        for p in range(NP):
            low_ahead(turn, p).wait_recv()
            at = pl.ds(p * PIECE, PIECE)
            middle[1, at] = (fetched[turn, 1, at].astype(F32) + known[1, at]).astype(BF16)
            rows = pl.ds(OWN - HALO + p * PIECE, PIECE)
            settle(0, rows, bottom_piece(middle.at[1], p, scales), term + 1)

            @pl.when(more)
            def _(p=p):
                high_edge(0, later, p).start()

        for p in range(NP):
            high_ahead(turn, p).wait_recv()
            at = pl.ds(p * PIECE, PIECE)
            middle[0, at] = (fetched[turn, 0, at].astype(F32) + known[0, at]).astype(BF16)
        for p in range(NP):
            settle(0, pl.ds(p * PIECE, PIECE), top_piece(middle.at[0], p, scales), term + 1)

            @pl.when(more)
            def _(p=p):
                low_edge(0, later, p).start()

        return carry

    lax.fori_loop(1, ROUNDS, double, 0)
    for p in range(NP):
        low_ahead(ROUNDS % 2, p).wait_send()
        high_ahead(ROUNDS % 2, p).wait_send()
    last = 0

    lane = lax.broadcasted_iota(jnp.int32, (HALO, BS), 1)
    strip = jnp.zeros((HALO, BS), F32)
    for g in range(W):
        turned = pltpu.roll(ybuf[last, g * HALO : (g + 1) * HALO], (NB * (g + 1)) % BS, 1)
        strip = jnp.where(lane // NB == g, turned, strip)
    packed[...] = strip.astype(BF16)
    edge = pltpu.make_async_remote_copy(
        src_ref=packed,
        dst_ref=arrived,
        send_sem=edge_sem.at[0],
        recv_sem=edge_sem.at[1],
        device_id=(after, row),
        device_id_type=MESH,
    )
    edge.start()
    edge.wait()
    @pl.when(cut == 0)
    def _():
        arrived[...] = jnp.zeros((HALO, BS), BF16)

    def share(src, slots, sent, got, peers):
        copies = []
        for o, peer in enumerate(peers):
            copies.append(
                pltpu.make_async_remote_copy(
                    src_ref=src,
                    dst_ref=slots.at[o],
                    send_sem=sent.at[o],
                    recv_sem=got.at[o],
                    device_id=(cut, peer),
                    device_id_type=MESH,
                )
            )
            copies[-1].start()
        return copies

    def collect(copies, own, slots):
        summed = own
        for o, copy in enumerate(copies):
            copy.wait()
            summed = summed + slots[o]
        return summed

    boundary = arrived[...]
    square = tdot(boundary, boundary)
    eight = BS // W // W
    group = lax.broadcasted_iota(jnp.int32, (eight, BS), 1) // NB
    gram = jnp.zeros((NB, BS), F32)
    for g in range(W):
        rows = square[g * NB : (g + 1) * NB]
        gram = gram + (pltpu.roll(rows, (BS - NB * g) % BS, 1) if g else rows)
    tight = jnp.zeros((eight, BS), F32)
    for g in range(W):
        rows = gram[g * eight : (g + 1) * eight]
        tight = jnp.where(group == g, pltpu.roll(rows, NB * g, 1) if g else rows, tight)
    gpart[...] = tight
    gram_z = share(gpart, gzin, gzsend, gzrecv, zpeers)
    cross = jnp.zeros((NB, BS), F32)
    for g in range(W):
        mine = vbuf[last, pl.ds(g * HALO, HALO)]
        cross = cross + tdot(boundary, mine)[g * NB : (g + 1) * NB]
    cpart[...] = cross
    cross_z = share(cpart, czin, czsend, czrecv, zpeers)
    gmid[...] = collect(gram_z, tight, gzin)
    gram_x = share(gmid, gxin, gxsend, gxrecv, xpeers)
    cmid[...] = collect(cross_z, cross, czin)
    cross_x = share(cmid, cxin, cxsend, cxrecv, xpeers)
    tight = collect(gram_x, gmid[...], gxin)

    across = lax.broadcasted_iota(jnp.int32, (NB, BS), 1)
    down = lax.broadcasted_iota(jnp.int32, (NB, BS), 0)
    loose = [tight if g == 0 else pltpu.roll(tight, BS - NB * g, 1) for g in range(W)]
    whole = jnp.where(across < NB, jnp.concatenate(loose, axis=0), 0.0)
    whole = whole + jnp.where((across == down) | (across == down + NB), 1.0, 0.0)
    for j in range(NB):
        row_j = whole[j : j + 1] * (1.0 / whole[j : j + 1, j : j + 1])
        whole = jnp.where(down == j, row_j, whole - whole[:, j : j + 1] * row_j)
    summed = collect(cross_x, cmid[...], cxin)
    tall = jnp.concatenate(
        [jnp.zeros((NB, BS), F32), summed, jnp.zeros((2 * NB, BS), F32)], axis=0
    )
    right = jnp.dot(whole, tall, preferred_element_type=F32, precision=lax.Precision.HIGHEST)
    solved = right.astype(BF16).astype(F32)
    for g in range(W):
        above_rows = [jnp.zeros((NB, BS), F32)] * g
        below_rows = [jnp.zeros((NB, BS), F32)] * (W - 1 - g)
        spread = jnp.concatenate([*above_rows, solved, *below_rows], axis=0).astype(BF16)
        correction = dot(boundary, spread)
        rows = pl.ds(g * HALO, HALO)
        out[rows] = (ybuf[last, rows] - correction).astype(BF16)


def body(nz, nx, ncut, vectors, blocks, block_cols, counts, lower_end, upper_end, coeffs):
    blocks = blocks.reshape(RB * MAXB, BS, BS)
    hbm = pl.BlockSpec(memory_space=pltpu.HBM)
    stage = pltpu.VMEM((W * MAXB + 1, BS, BS), BF16)
    dma = pltpu.SemaphoreType.DMA
    return pl.pallas_call(
        functools.partial(kernel, nz, nx, ncut),
        out_shape=pltpu.VMEM((OWN, BS), BF16),
        in_specs=[hbm] * 7,
        out_specs=pl.BlockSpec(memory_space=pltpu.VMEM),
        scratch_shapes=[
            pltpu.SMEM((MAXB, RB), jnp.int32),
            pltpu.SMEM((RB,), jnp.int32),
            pltpu.SMEM((1,), F32),
            pltpu.SMEM((1,), F32),
            pltpu.SMEM((1, DEG + 1), F32),
            stage,
            stage,
            stage,
            stage,
            pltpu.VMEM((QUADS, HALO, WIDE), BF16),
            pltpu.VMEM((2, OWN, BS), BF16),
            pltpu.VMEM((2, OWN, BS), F32),
            pltpu.VMEM((OWN, BS), F32),
            pltpu.VMEM((OWN, BS), BF16),
            pltpu.VMEM((HALO, BS), BF16),
            pltpu.VMEM((HALO, BS), BF16),
            pltpu.VMEM((2, HALO, BS), F32),
            pltpu.VMEM((2, 2, HALO, BS), BF16),
            pltpu.VMEM((2, HALO, BS), BF16),
            pltpu.VMEM((2, 2, HALO, BS), BF16),
            pltpu.VMEM((2, HALO, BS), F32),
            pltpu.VMEM((2, HALO, BS), F32),
            pltpu.VMEM((2, HALO, BS), BF16),
            pltpu.VMEM((2, HALO, HALO), BF16),
            pltpu.VMEM((8, BS), F32),
            pltpu.VMEM((nz - 1, 8, BS), F32),
            pltpu.VMEM((8, BS), F32),
            pltpu.VMEM((nx - 1, 8, BS), F32),
            pltpu.VMEM((NB, BS), F32),
            pltpu.VMEM((nz - 1, NB, BS), F32),
            pltpu.VMEM((NB, BS), F32),
            pltpu.VMEM((nx - 1, NB, BS), F32),
            dma((5,)),
            dma((QUADS,)),
            dma,
            *[dma((2, 2, NP))] * 4,
            *[dma((2, W))] * 4,
            dma((2,)),
            *[dma((n,)) for n in 2 * [nz - 1, nz - 1, nx - 1, nx - 1]],
        ],
        compiler_params=pltpu.CompilerParams(
            collective_id=0, has_side_effects=True, vmem_limit_bytes=59 * 1024 * 1024
        ),
    )(vectors, blocks, block_cols.T, counts, lower_end, upper_end, coeffs)


def solution(mesh):
    rows = mesh.shape["rows"]
    nx = 4 if rows == 32 else 2
    return jax.shard_map(
        functools.partial(body, rows // nx, nx, mesh.shape["cuts"]),
        mesh=mesh,
        in_specs=(
            P("rows", "cuts"),
            P("rows", None, None, None),
            P("rows", None),
            P("rows"),
            P("cuts"),
            P("cuts"),
            P("cuts", None),
        ),
        out_specs=P("rows", "cuts"),
        check_vma=False,
    )
```

```python
import functools

import jax
import jax.numpy as jnp
from jax import lax
from jax.experimental import pallas as pl
from jax.experimental.pallas import tpu as pltpu
from jax.sharding import PartitionSpec as P

BS = 128
MAXB = 8
W = 4
DEG = 6
PASSES = 2
NB = 32
RB = 16
HALO = W * BS
NP = 2
PIECE = HALO // NP
ROUNDS = PASSES * DEG // 2
OWN = RB * BS
QUADS = RB // W
WIDE = 3 * W * BS
MESH = pl.DeviceIdType.MESH
F32 = jnp.float32
BF16 = jnp.bfloat16


def dot(a, b):
    return jnp.dot(a, b, preferred_element_type=F32)


def tdot(a, b):
    return lax.dot_general(a, b, (((0,), (0,)), ((), ())), preferred_element_type=F32)


def kernel(
    nz,
    nx,
    ncut,
    vec,
    blocks,
    cols_in,
    counts_in,
    lower_in,
    upper_in,
    coeffs_in,
    out,
    cols,
    counts,
    lower,
    upper,
    coeffs,
    stage0,
    stage1,
    stage2,
    stage3,
    dense,
    vbuf,
    ybuf,
    total,
    start,
    packed,
    arrived,
    acc,
    halo,
    ahead,
    fetched,
    known,
    early,
    middle,
    corner,
    gpart,
    gzin,
    gmid,
    gxin,
    cpart,
    czin,
    cmid,
    cxin,
    small_sem,
    block_sem,
    vec_sem,
    send_sem,
    recv_sem,
    asend,
    arecv,
    csend,
    crecv,
    wsend,
    wrecv,
    edge_sem,
    gzsend,
    gzrecv,
    gxsend,
    gxrecv,
    czsend,
    czrecv,
    cxsend,
    cxrecv,
):
    stages = (stage0, stage1, stage2, stage3)
    row = lax.axis_index("rows")
    cut = lax.axis_index("cuts")
    nrow = nz * nx
    z = lax.rem(row, nz)
    x = lax.div(row, nz)
    low = lax.rem(row + nrow - 1, nrow)
    high = lax.rem(row + 1, nrow)
    after = lax.rem(cut + 1, ncut)
    before = lax.rem(cut + ncut - 1, ncut)
    zpeers = [x * nz + lax.rem(z + o, nz) for o in range(1, nz)]
    xpeers = [lax.rem(x + o, nx) * nz + z for o in range(1, nx)]

    vec_copy = pltpu.make_async_copy(vec, start, vec_sem)
    vec_copy.start()
    small = []
    for n, (src, dst) in enumerate(
        ((lower_in, lower), (upper_in, upper), (coeffs_in, coeffs), (cols_in, cols), (counts_in, counts))
    ):
        small.append(pltpu.make_async_copy(src, dst, small_sem.at[n]))
        small[-1].start()
    block_copies = []
    for q in range(QUADS):
        copy = pltpu.make_async_copy(
            blocks.at[pl.ds(q * W * MAXB, W * MAXB)],
            stages[q].at[pl.ds(0, W * MAXB)],
            block_sem.at[q],
        )
        copy.start()
        block_copies.append(copy)

    corner[...] = jnp.zeros((2, HALO, HALO), BF16)
    barrier = pltpu.get_barrier_semaphore()
    greeted = 0
    for other in [low, high, *zpeers, *xpeers]:
        pl.semaphore_signal(barrier, inc=1, device_id=(cut, other), device_id_type=MESH)
        greeted += 1
    for other in (before, after):
        pl.semaphore_signal(barrier, inc=1, device_id=(other, row), device_id_type=MESH)
        greeted += 1

    for q in range(QUADS):
        dense[q] = jnp.zeros((W * BS, WIDE), BF16)
        stages[q][W * MAXB] = jnp.zeros((BS, BS), BF16)
    for copy in small:
        copy.wait()
    centre = (lower[0] + upper[0]) * 0.5
    half = (upper[0] - lower[0]) * 0.5
    inverse = 1.0 / half

    pl.semaphore_wait(barrier, greeted)

    def side_copy(src, dst, sent, got, device):
        return pltpu.make_async_remote_copy(
            src_ref=src,
            dst_ref=dst,
            send_sem=sent,
            recv_sem=got,
            device_id=(cut, device),
            device_id_type=MESH,
        )

    def to_low(src, turn, p):
        return side_copy(
            src,
            halo.at[turn, 1, pl.ds(p * PIECE, PIECE)],
            send_sem.at[0, turn, p],
            recv_sem.at[1, turn, p],
            low,
        )

    def to_high(src, turn, p):
        return side_copy(
            src,
            halo.at[turn, 0, pl.ds(p * PIECE, PIECE)],
            send_sem.at[1, turn, p],
            recv_sem.at[0, turn, p],
            high,
        )

    def low_edge(slot, turn, p):
        return to_low(vbuf.at[slot, pl.ds(p * PIECE, PIECE)], turn, p)

    def high_edge(slot, turn, p):
        return to_high(vbuf.at[slot, pl.ds(OWN - HALO + p * PIECE, PIECE)], turn, p)

    def low_ahead(turn, p):
        at = pl.ds(p * PIECE, PIECE)
        return side_copy(
            ahead.at[0, at],
            fetched.at[turn, 1, at],
            asend.at[0, turn, p],
            arecv.at[1, turn, p],
            low,
        )

    def high_ahead(turn, p):
        at = pl.ds(p * PIECE, PIECE)
        return side_copy(
            ahead.at[1, at],
            fetched.at[turn, 0, at],
            asend.at[1, turn, p],
            arecv.at[0, turn, p],
            high,
        )

    def low_corner(i):
        at, lanes = pl.ds(i * BS, BS), pl.ds(i * BS, (W - i) * BS)
        return side_copy(
            dense.at[0, at, lanes], corner.at[1, at, lanes], csend.at[0, i], crecv.at[1, i], low
        )

    def high_corner(i):
        at, lanes = pl.ds(i * BS, BS), pl.ds(0, (i + 1) * BS)
        return side_copy(
            dense.at[QUADS - 1, at, pl.ds(2 * HALO, (i + 1) * BS)],
            corner.at[0, at, lanes],
            csend.at[1, i],
            crecv.at[0, i],
            high,
        )

    def swapped(side, i):
        at = pl.ds(i * BS, BS)
        lanes = pl.ds(i * BS, (W - i) * BS) if side else pl.ds(0, (i + 1) * BS)
        return pltpu.make_async_remote_copy(
            src_ref=corner.at[side, at, lanes],
            dst_ref=corner.at[side, at, lanes],
            send_sem=wsend.at[side, i],
            recv_sem=wrecv.at[side, i],
            device_id=(cut + 1 - 2 * lax.rem(cut, 2), row),
            device_id_type=MESH,
        )

    halves = ((0, (0, W - 1)), (1, (1, W - 2)))

    for p in range(NP):
        to_high(vec.at[pl.ds(OWN - HALO + p * PIECE, PIECE)], 0, p).start()
        to_low(vec.at[pl.ds(p * PIECE, PIECE)], 0, p).start()

    vec_copy.wait()
    vbuf[0] = start[...]
    first = start[...].astype(F32)
    ybuf[0] = first
    ybuf[1] = jnp.zeros((OWN, BS), F32)
    total[...] = coeffs[0, 0] * first

    for q in range(QUADS):
        block_copies[q].wait()

        def place(i, carry, q=q):
            r = q * W + i
            base = row * RB + r - W
            live = counts[r]
            near = [jnp.where(s < live, cols[s, r] - base, -1) for s in range(MAXB)]
            for d in range(2 * W + 1):
                slot = jnp.int32(W * MAXB)
                for s in range(MAXB):
                    slot = jnp.where(near[s] == d, i * MAXB + s, slot)
                rows = pl.ds(pl.multiple_of(i * BS, BS), BS)
                lanes = pl.ds(pl.multiple_of((i + d) * BS, BS), BS)
                dense[q, rows, lanes] = stages[q][slot]
            return carry

        lax.fori_loop(0, W, place, 0)

    def factors(term):
        opening = term == 0
        scale = jnp.where(opening, 1.0, 2.0) * inverse
        return scale, scale * centre, jnp.where(opening, 0.0, 1.0)

    def recur(now, new, rows, product, scales):
        scale, shift, keep = scales
        return scale * product - shift * ybuf[now, rows] - keep * ybuf[new, rows]

    def settle(new, rows, upcoming, term):
        closing = term == DEG - 1
        summed = total[rows] + coeffs[0, term + 1] * upcoming
        value = jnp.where(closing, summed, upcoming)
        total[rows] = jnp.where(closing, coeffs[0, 0] * summed, summed)
        ybuf[new, rows] = value
        vbuf[new, rows] = value.astype(BF16)

    def inner(now, new, term, scales):
        pair = 2 * BS
        wide = (2 * W + 2) * BS
        for q in (1, 2):
            for j in (0, 1):
                at = q * HALO + j * pair
                product = dot(
                    dense[q, j * pair : (j + 1) * pair, j * pair : j * pair + wide],
                    vbuf[now, pl.ds(at - HALO, wide)],
                )
                rows = pl.ds(at, pair)
                settle(new, rows, recur(now, new, rows, product, scales), term)

    top, bottom = pl.ds(0, HALO), pl.ds(OWN - HALO, HALO)

    def own_part(now, new, scales):
        product = dot(dense[QUADS - 1, :, : 2 * HALO], vbuf[now, pl.ds(OWN - 2 * HALO, 2 * HALO)])
        acc[1] = recur(now, new, bottom, product, scales)
        product = dot(dense[0, :, HALO:], vbuf[now, pl.ds(0, 2 * HALO)])
        acc[0] = recur(now, new, top, product, scales)

    def bottom_piece(src, p, scales):
        inside = slice(p * PIECE, (p + 1) * PIECE)
        deep = (p + 1) * PIECE
        product = dot(dense[QUADS - 1, inside, 2 * HALO : 2 * HALO + deep], src[pl.ds(0, deep)])
        return acc[1, inside] + scales[0] * product

    def top_piece(src, p, scales):
        inside = slice(p * PIECE, (p + 1) * PIECE)
        product = dot(
            dense[0, inside, p * PIECE : HALO], src[pl.ds(p * PIECE, HALO - p * PIECE)]
        )
        return acc[0, inside] + scales[0] * product

    def edges(new, turn):
        return [f(new, turn, p) for f in (high_edge, low_edge) for p in range(NP)]

    def step(k, carry):
        now = lax.rem(k, 2)
        new = 1 - now
        scales = factors(k)
        own_part(now, new, scales)
        inner(now, new, k, scales)

        @pl.when(k > 0)
        def _():
            for copy in edges(new, new):
                copy.wait_send()

        for p in range(NP):
            low_edge(now, now, p).wait_recv()
            settle(
                new,
                pl.ds(OWN - HALO + p * PIECE, PIECE),
                bottom_piece(halo.at[now, 1], p, scales),
                k,
            )
            high_edge(new, new, p).start()
        for p in range(NP):
            high_edge(now, now, p).wait_recv()
        for p in range(NP):
            settle(new, pl.ds(p * PIECE, PIECE), top_piece(halo.at[now, 0], p, scales), k)
            low_edge(new, new, p).start()
        return carry

    lax.fori_loop(0, 1, step, 0)
    for parity, mine in halves:

        @pl.when(lax.rem(cut, 2) == parity)
        def _(mine=mine):
            for i in mine:
                high_corner(i).start()
                low_corner(i).start()

    lax.fori_loop(1, 2, step, 0)
    for parity, mine in halves:

        @pl.when(lax.rem(cut, 2) == parity)
        def _(mine=mine):
            for i in mine:
                for copy in (high_corner(i), low_corner(i)):
                    copy.wait()
                for side in (0, 1):
                    swapped(side, i).start()

    for copy in edges(1, 1):
        copy.wait_send()

    low_half = HALO // 2
    groups = (
        tuple(HALO + g * low_half for g in range(W)),
        (0, low_half, OWN - HALO, OWN - low_half),
    )
    lane = lax.broadcasted_iota(jnp.int32, (low_half, BS), 1)

    def boundary_half(h):
        at = pl.ds(h * low_half, low_half)
        return pltpu.make_async_remote_copy(
            src_ref=packed.at[at],
            dst_ref=arrived.at[at],
            send_sem=edge_sem.at[0, h],
            recv_sem=edge_sem.at[1, h],
            device_id=(after, row),
            device_id_type=MESH,
        )

    def send_boundary(h):
        strip = jnp.zeros((low_half, BS), F32)
        for g, first_row in enumerate(groups[h]):
            turned = pltpu.roll(ybuf[0, pl.ds(first_row, low_half)], (NB * (g + 1)) % BS, 1)
            strip = jnp.where(lane // NB == g, turned, strip)
        packed[pl.ds(h * low_half, low_half)] = strip.astype(BF16)
        boundary_half(h).start()

    def double(j, carry):
        turn = lax.rem(j + 1, 2)
        later = 1 - turn
        term = lax.rem(2 * j, DEG)
        scales = factors(term)

        @pl.when(j > 1)
        def _():
            for p in range(NP):
                low_ahead(later, p).wait_send()
                high_ahead(later, p).wait_send()

        own_part(0, 1, scales)
        ahead[1] = acc[1].astype(BF16)
        for p in range(NP):
            high_ahead(turn, p).start()
        ahead[0] = acc[0].astype(BF16)
        for p in range(NP):
            low_ahead(turn, p).start()
        inner(0, 1, term, scales)
        early[1] = dot(dense[QUADS - 1, :, :HALO], vbuf[1, pl.ds(OWN - 2 * HALO, HALO)])
        early[0] = dot(dense[0, :, 2 * HALO :], vbuf[1, pl.ds(HALO, HALO)])

        @pl.when(j == 1)
        def _():
            for parity, mine in halves:
                other = halves[1 - parity][1]

                @pl.when(lax.rem(cut, 2) == parity)
                def _(mine=mine, other=other):
                    for side in (0, 1):
                        for i in mine:
                            swapped(side, i).wait_send()
                        for i in other:
                            swapped(side, i).wait_recv()

        known[1] = scales[0] * dot(corner[1], vbuf[0, bottom])
        known[0] = scales[0] * dot(corner[0], vbuf[0, top])
        for p in range(NP):
            low_edge(0, turn, p).wait_recv()
        product = dot(dense[QUADS - 1, :, 2 * HALO :], halo[turn, 1])
        settle(1, bottom, acc[1] + scales[0] * product, term)
        scales = factors(term + 1)
        product = early[1] + dot(dense[QUADS - 1, :, HALO : 2 * HALO], vbuf[1, bottom])
        acc[1] = recur(1, 0, bottom, product, scales)
        for p in range(NP):
            high_edge(0, turn, p).wait_recv()
        product = dot(dense[0, :, :HALO], halo[turn, 0])
        settle(1, top, acc[0] + factors(term)[0] * product, term)
        product = early[0] + dot(dense[0, :, HALO : 2 * HALO], vbuf[1, top])
        acc[0] = recur(1, 0, top, product, scales)
        for copy in edges(0, turn):
            copy.wait_send()
        more = j < ROUNDS - 1

        inner(1, 0, term + 1, scales)

        @pl.when(jnp.logical_not(more))
        def _():
            send_boundary(0)

        for p in range(NP):
            low_ahead(turn, p).wait_recv()
            at = pl.ds(p * PIECE, PIECE)
            middle[1, at] = (fetched[turn, 1, at].astype(F32) + known[1, at]).astype(BF16)
            rows = pl.ds(OWN - HALO + p * PIECE, PIECE)
            settle(0, rows, bottom_piece(middle.at[1], p, scales), term + 1)

            @pl.when(more)
            def _(p=p):
                high_edge(0, later, p).start()

        for p in range(NP):
            high_ahead(turn, p).wait_recv()
            at = pl.ds(p * PIECE, PIECE)
            middle[0, at] = (fetched[turn, 0, at].astype(F32) + known[0, at]).astype(BF16)
        for p in range(NP):
            settle(0, pl.ds(p * PIECE, PIECE), top_piece(middle.at[0], p, scales), term + 1)

            @pl.when(more)
            def _(p=p):
                low_edge(0, later, p).start()

        return carry

    lax.fori_loop(1, ROUNDS, double, 0)
    for p in range(NP):
        low_ahead(ROUNDS % 2, p).wait_send()
        high_ahead(ROUNDS % 2, p).wait_send()
    last = 0

    send_boundary(1)
    square = jnp.zeros((BS, BS), F32)
    cross = jnp.zeros((NB, BS), F32)
    for h in (0, 1):
        boundary_half(h).wait()
        at = pl.ds(h * low_half, low_half)

        @pl.when(cut == 0)
        def _(at=at):
            arrived[at] = jnp.zeros((low_half, BS), BF16)

        boundary = arrived[at]
        square = square + tdot(boundary, boundary)
        for g, first_row in enumerate(groups[h]):
            mine = vbuf[last, pl.ds(first_row, low_half)]
            cross = cross + tdot(boundary, mine)[g * NB : (g + 1) * NB]

    def share(src, slots, sent, got, peers):
        copies = []
        for o, peer in enumerate(peers):
            copies.append(
                pltpu.make_async_remote_copy(
                    src_ref=src,
                    dst_ref=slots.at[o],
                    send_sem=sent.at[o],
                    recv_sem=got.at[o],
                    device_id=(cut, peer),
                    device_id_type=MESH,
                )
            )
            copies[-1].start()
        return copies

    def collect(copies, own, slots):
        summed = own
        for o, copy in enumerate(copies):
            copy.wait()
            summed = summed + slots[o]
        return summed

    eight = BS // W // W
    group = lax.broadcasted_iota(jnp.int32, (eight, BS), 1) // NB
    gram = jnp.zeros((NB, BS), F32)
    for g in range(W):
        rows = square[g * NB : (g + 1) * NB]
        gram = gram + (pltpu.roll(rows, (BS - NB * g) % BS, 1) if g else rows)
    tight = jnp.zeros((eight, BS), F32)
    for g in range(W):
        rows = gram[g * eight : (g + 1) * eight]
        tight = jnp.where(group == g, pltpu.roll(rows, NB * g, 1) if g else rows, tight)
    gpart[...] = tight
    gram_z = share(gpart, gzin, gzsend, gzrecv, zpeers)
    cpart[...] = cross
    cross_z = share(cpart, czin, czsend, czrecv, zpeers)
    gmid[...] = collect(gram_z, tight, gzin)
    gram_x = share(gmid, gxin, gxsend, gxrecv, xpeers)
    cmid[...] = collect(cross_z, cross, czin)
    cross_x = share(cmid, cxin, cxsend, cxrecv, xpeers)
    tight = collect(gram_x, gmid[...], gxin)

    across = lax.broadcasted_iota(jnp.int32, (NB, BS), 1)
    down = lax.broadcasted_iota(jnp.int32, (NB, BS), 0)
    loose = [tight if g == 0 else pltpu.roll(tight, BS - NB * g, 1) for g in range(W)]
    whole = jnp.where(across < NB, jnp.concatenate(loose, axis=0), 0.0)
    whole = whole + jnp.where((across == down) | (across == down + NB), 1.0, 0.0)
    for j in range(NB):
        row_j = whole[j : j + 1] * (1.0 / whole[j : j + 1, j : j + 1])
        whole = jnp.where(down == j, row_j, whole - whole[:, j : j + 1] * row_j)
    summed = collect(cross_x, cmid[...], cxin)
    tall = jnp.concatenate(
        [jnp.zeros((NB, BS), F32), summed, jnp.zeros((2 * NB, BS), F32)], axis=0
    )
    right = jnp.dot(whole, tall, preferred_element_type=F32, precision=lax.Precision.HIGHEST)
    solved = right.astype(BF16).astype(F32)
    for g in range(W):
        above_rows = [jnp.zeros((NB, BS), F32)] * g
        below_rows = [jnp.zeros((NB, BS), F32)] * (W - 1 - g)
        spread = jnp.concatenate([*above_rows, solved, *below_rows], axis=0).astype(BF16)
        for h in (0, 1):
            correction = dot(arrived[pl.ds(h * low_half, low_half)], spread)
            rows = pl.ds(groups[h][g], low_half)
            out[rows] = (ybuf[last, rows] - correction).astype(BF16)


def body(nz, nx, ncut, vectors, blocks, block_cols, counts, lower_end, upper_end, coeffs):
    blocks = blocks.reshape(RB * MAXB, BS, BS)
    hbm = pl.BlockSpec(memory_space=pltpu.HBM)
    stage = pltpu.VMEM((W * MAXB + 1, BS, BS), BF16)
    dma = pltpu.SemaphoreType.DMA
    return pl.pallas_call(
        functools.partial(kernel, nz, nx, ncut),
        out_shape=pltpu.VMEM((OWN, BS), BF16),
        in_specs=[hbm] * 7,
        out_specs=pl.BlockSpec(memory_space=pltpu.VMEM),
        scratch_shapes=[
            pltpu.SMEM((MAXB, RB), jnp.int32),
            pltpu.SMEM((RB,), jnp.int32),
            pltpu.SMEM((1,), F32),
            pltpu.SMEM((1,), F32),
            pltpu.SMEM((1, DEG + 1), F32),
            stage,
            stage,
            stage,
            stage,
            pltpu.VMEM((QUADS, HALO, WIDE), BF16),
            pltpu.VMEM((2, OWN, BS), BF16),
            pltpu.VMEM((2, OWN, BS), F32),
            pltpu.VMEM((OWN, BS), F32),
            pltpu.VMEM((OWN, BS), BF16),
            pltpu.VMEM((HALO, BS), BF16),
            pltpu.VMEM((HALO, BS), BF16),
            pltpu.VMEM((2, HALO, BS), F32),
            pltpu.VMEM((2, 2, HALO, BS), BF16),
            pltpu.VMEM((2, HALO, BS), BF16),
            pltpu.VMEM((2, 2, HALO, BS), BF16),
            pltpu.VMEM((2, HALO, BS), F32),
            pltpu.VMEM((2, HALO, BS), F32),
            pltpu.VMEM((2, HALO, BS), BF16),
            pltpu.VMEM((2, HALO, HALO), BF16),
            pltpu.VMEM((8, BS), F32),
            pltpu.VMEM((nz - 1, 8, BS), F32),
            pltpu.VMEM((8, BS), F32),
            pltpu.VMEM((nx - 1, 8, BS), F32),
            pltpu.VMEM((NB, BS), F32),
            pltpu.VMEM((nz - 1, NB, BS), F32),
            pltpu.VMEM((NB, BS), F32),
            pltpu.VMEM((nx - 1, NB, BS), F32),
            dma((5,)),
            dma((QUADS,)),
            dma,
            *[dma((2, 2, NP))] * 4,
            *[dma((2, W))] * 4,
            dma((2, 2)),
            *[dma((n,)) for n in 2 * [nz - 1, nz - 1, nx - 1, nx - 1]],
        ],
        compiler_params=pltpu.CompilerParams(
            collective_id=0, has_side_effects=True, vmem_limit_bytes=59 * 1024 * 1024
        ),
    )(vectors, blocks, block_cols.T, counts, lower_end, upper_end, coeffs)


def solution(mesh):
    rows = mesh.shape["rows"]
    nx = 4 if rows == 32 else 2
    return jax.shard_map(
        functools.partial(body, rows // nx, nx, mesh.shape["cuts"]),
        mesh=mesh,
        in_specs=(
            P("rows", "cuts"),
            P("rows", None, None, None),
            P("rows", None),
            P("rows"),
            P("cuts"),
            P("cuts"),
            P("cuts", None),
        ),
        out_specs=P("rows", "cuts"),
        check_vma=False,
    )
```

```python
import functools

import jax
import jax.numpy as jnp
from jax import lax
from jax.experimental import pallas as pl
from jax.experimental.pallas import tpu as pltpu
from jax.sharding import PartitionSpec as P

BS = 128
MAXB = 8
W = 4
DEG = 6
PASSES = 2
NB = 32
RB = 16
HALO = W * BS
NP = 2
PIECE = HALO // NP
ROUNDS = PASSES * DEG // 2
OWN = RB * BS
QUADS = RB // W
WIDE = 3 * W * BS
MESH = pl.DeviceIdType.MESH
F32 = jnp.float32
BF16 = jnp.bfloat16


def dot(a, b):
    return jnp.dot(a, b, preferred_element_type=F32)


def tdot(a, b):
    return lax.dot_general(a, b, (((0,), (0,)), ((), ())), preferred_element_type=F32)


def kernel(
    nz,
    nx,
    ncut,
    vec,
    blocks,
    cols_in,
    counts_in,
    lower_in,
    upper_in,
    coeffs_in,
    out,
    cols,
    counts,
    lower,
    upper,
    coeffs,
    stage0,
    stage1,
    stage2,
    stage3,
    dense,
    vbuf,
    ybuf,
    total,
    start,
    packed,
    arrived,
    acc,
    halo,
    ahead,
    fetched,
    known,
    early,
    middle,
    corner,
    gpart,
    gzin,
    gmid,
    gxin,
    cpart,
    czin,
    cmid,
    cxin,
    small_sem,
    block_sem,
    vec_sem,
    send_sem,
    recv_sem,
    asend,
    arecv,
    csend,
    crecv,
    wsend,
    wrecv,
    edge_sem,
    gzsend,
    gzrecv,
    gxsend,
    gxrecv,
    czsend,
    czrecv,
    cxsend,
    cxrecv,
):
    stages = (stage0, stage1, stage2, stage3)
    row = lax.axis_index("rows")
    cut = lax.axis_index("cuts")
    nrow = nz * nx
    z = lax.rem(row, nz)
    x = lax.div(row, nz)
    low = lax.rem(row + nrow - 1, nrow)
    high = lax.rem(row + 1, nrow)
    after = lax.rem(cut + 1, ncut)
    before = lax.rem(cut + ncut - 1, ncut)
    zpeers = [x * nz + lax.rem(z + o, nz) for o in range(1, nz)]
    xpeers = [lax.rem(x + o, nx) * nz + z for o in range(1, nx)]

    vec_copy = pltpu.make_async_copy(vec, start, vec_sem)
    vec_copy.start()
    small = []
    for n, (src, dst) in enumerate(
        ((lower_in, lower), (upper_in, upper), (coeffs_in, coeffs), (cols_in, cols), (counts_in, counts))
    ):
        small.append(pltpu.make_async_copy(src, dst, small_sem.at[n]))
        small[-1].start()
    block_copies = []
    for q in range(QUADS):
        copy = pltpu.make_async_copy(
            blocks.at[pl.ds(q * W * MAXB, W * MAXB)],
            stages[q].at[pl.ds(0, W * MAXB)],
            block_sem.at[q],
        )
        copy.start()
        block_copies.append(copy)

    corner[...] = jnp.zeros((2, HALO, HALO), BF16)
    barrier = pltpu.get_barrier_semaphore()
    greeted = 0
    for other in [low, high, *zpeers, *xpeers]:
        pl.semaphore_signal(barrier, inc=1, device_id=(cut, other), device_id_type=MESH)
        greeted += 1
    for other in (before, after):
        pl.semaphore_signal(barrier, inc=1, device_id=(other, row), device_id_type=MESH)
        greeted += 1

    for q in range(QUADS):
        dense[q] = jnp.zeros((W * BS, WIDE), BF16)
        stages[q][W * MAXB] = jnp.zeros((BS, BS), BF16)
    for copy in small:
        copy.wait()
    centre = (lower[0] + upper[0]) * 0.5
    half = (upper[0] - lower[0]) * 0.5
    inverse = 1.0 / half

    pl.semaphore_wait(barrier, greeted)

    def side_copy(src, dst, sent, got, device):
        return pltpu.make_async_remote_copy(
            src_ref=src,
            dst_ref=dst,
            send_sem=sent,
            recv_sem=got,
            device_id=(cut, device),
            device_id_type=MESH,
        )

    def to_low(src, turn, p):
        return side_copy(
            src,
            halo.at[turn, 1, pl.ds(p * PIECE, PIECE)],
            send_sem.at[0, turn, p],
            recv_sem.at[1, turn, p],
            low,
        )

    def to_high(src, turn, p):
        return side_copy(
            src,
            halo.at[turn, 0, pl.ds(p * PIECE, PIECE)],
            send_sem.at[1, turn, p],
            recv_sem.at[0, turn, p],
            high,
        )

    def low_edge(slot, turn, p):
        return to_low(vbuf.at[slot, pl.ds(p * PIECE, PIECE)], turn, p)

    def high_edge(slot, turn, p):
        return to_high(vbuf.at[slot, pl.ds(OWN - HALO + p * PIECE, PIECE)], turn, p)

    def low_ahead(turn, p):
        at = pl.ds(p * PIECE, PIECE)
        return side_copy(
            ahead.at[0, at],
            fetched.at[turn, 1, at],
            asend.at[0, turn, p],
            arecv.at[1, turn, p],
            low,
        )

    def high_ahead(turn, p):
        at = pl.ds(p * PIECE, PIECE)
        return side_copy(
            ahead.at[1, at],
            fetched.at[turn, 0, at],
            asend.at[1, turn, p],
            arecv.at[0, turn, p],
            high,
        )

    def low_corner(i):
        at, lanes = pl.ds(i * BS, BS), pl.ds(i * BS, (W - i) * BS)
        return side_copy(
            dense.at[0, at, lanes], corner.at[1, at, lanes], csend.at[0, i], crecv.at[1, i], low
        )

    def high_corner(i):
        at, lanes = pl.ds(i * BS, BS), pl.ds(0, (i + 1) * BS)
        return side_copy(
            dense.at[QUADS - 1, at, pl.ds(2 * HALO, (i + 1) * BS)],
            corner.at[0, at, lanes],
            csend.at[1, i],
            crecv.at[0, i],
            high,
        )

    def swapped(side, i):
        at = pl.ds(i * BS, BS)
        lanes = pl.ds(i * BS, (W - i) * BS) if side else pl.ds(0, (i + 1) * BS)
        return pltpu.make_async_remote_copy(
            src_ref=corner.at[side, at, lanes],
            dst_ref=corner.at[side, at, lanes],
            send_sem=wsend.at[side, i],
            recv_sem=wrecv.at[side, i],
            device_id=(cut + 1 - 2 * lax.rem(cut, 2), row),
            device_id_type=MESH,
        )

    halves = ((0, (0, W - 1)), (1, (1, W - 2)))

    for p in range(NP):
        to_high(vec.at[pl.ds(OWN - HALO + p * PIECE, PIECE)], 0, p).start()
        to_low(vec.at[pl.ds(p * PIECE, PIECE)], 0, p).start()

    vec_copy.wait()
    vbuf[0] = start[...]
    first = start[...].astype(F32)
    ybuf[0] = first
    ybuf[1] = jnp.zeros((OWN, BS), F32)
    total[...] = coeffs[0, 0] * first

    for q in range(QUADS):
        block_copies[q].wait()

        def place(i, carry, q=q):
            r = q * W + i
            base = row * RB + r - W
            live = counts[r]
            near = [jnp.where(s < live, cols[s, r] - base, -1) for s in range(MAXB)]
            for d in range(2 * W + 1):
                slot = jnp.int32(W * MAXB)
                for s in range(MAXB):
                    slot = jnp.where(near[s] == d, i * MAXB + s, slot)
                rows = pl.ds(pl.multiple_of(i * BS, BS), BS)
                lanes = pl.ds(pl.multiple_of((i + d) * BS, BS), BS)
                dense[q, rows, lanes] = stages[q][slot]
            return carry

        lax.fori_loop(0, W, place, 0)

    def factors(term):
        opening = term == 0
        scale = jnp.where(opening, 1.0, 2.0) * inverse
        return scale, scale * centre, jnp.where(opening, 0.0, 1.0)

    def recur(now, new, rows, product, scales):
        scale, shift, keep = scales
        return scale * product - shift * ybuf[now, rows] - keep * ybuf[new, rows]

    def settle(new, rows, upcoming, term):
        closing = term == DEG - 1
        summed = total[rows] + coeffs[0, term + 1] * upcoming
        value = jnp.where(closing, summed, upcoming)
        total[rows] = jnp.where(closing, coeffs[0, 0] * summed, summed)
        ybuf[new, rows] = value
        vbuf[new, rows] = value.astype(BF16)

    def inner(now, new, term, scales):
        wide = (2 * W + 1) * BS
        for q in (1, 2):
            for i in range(W):
                at = q * HALO + i * BS
                product = dot(
                    dense[q, i * BS : (i + 1) * BS, i * BS : i * BS + wide],
                    vbuf[now, pl.ds(at - HALO, wide)],
                )
                rows = pl.ds(at, BS)
                settle(new, rows, recur(now, new, rows, product, scales), term)

    top, bottom = pl.ds(0, HALO), pl.ds(OWN - HALO, HALO)

    def own_part(now, new, scales):
        product = dot(dense[QUADS - 1, :, : 2 * HALO], vbuf[now, pl.ds(OWN - 2 * HALO, 2 * HALO)])
        acc[1] = recur(now, new, bottom, product, scales)
        product = dot(dense[0, :, HALO:], vbuf[now, pl.ds(0, 2 * HALO)])
        acc[0] = recur(now, new, top, product, scales)

    def bottom_piece(src, p, scales):
        inside = slice(p * PIECE, (p + 1) * PIECE)
        deep = (p + 1) * PIECE
        product = dot(dense[QUADS - 1, inside, 2 * HALO : 2 * HALO + deep], src[pl.ds(0, deep)])
        return acc[1, inside] + scales[0] * product

    def top_piece(src, p, scales):
        inside = slice(p * PIECE, (p + 1) * PIECE)
        product = dot(
            dense[0, inside, p * PIECE : HALO], src[pl.ds(p * PIECE, HALO - p * PIECE)]
        )
        return acc[0, inside] + scales[0] * product

    def edges(new, turn):
        return [f(new, turn, p) for f in (high_edge, low_edge) for p in range(NP)]

    def step(k, carry):
        now = lax.rem(k, 2)
        new = 1 - now
        scales = factors(k)
        own_part(now, new, scales)
        inner(now, new, k, scales)

        @pl.when(k > 0)
        def _():
            for copy in edges(new, new):
                copy.wait_send()

        for p in range(NP):
            low_edge(now, now, p).wait_recv()
            settle(
                new,
                pl.ds(OWN - HALO + p * PIECE, PIECE),
                bottom_piece(halo.at[now, 1], p, scales),
                k,
            )
            high_edge(new, new, p).start()
        for p in range(NP):
            high_edge(now, now, p).wait_recv()
        for p in range(NP):
            settle(new, pl.ds(p * PIECE, PIECE), top_piece(halo.at[now, 0], p, scales), k)
            low_edge(new, new, p).start()
        return carry

    lax.fori_loop(0, 1, step, 0)
    for parity, mine in halves:

        @pl.when(lax.rem(cut, 2) == parity)
        def _(mine=mine):
            for i in mine:
                high_corner(i).start()
                low_corner(i).start()

    lax.fori_loop(1, 2, step, 0)
    for parity, mine in halves:

        @pl.when(lax.rem(cut, 2) == parity)
        def _(mine=mine):
            for i in mine:
                for copy in (high_corner(i), low_corner(i)):
                    copy.wait()
                for side in (0, 1):
                    swapped(side, i).start()

    for copy in edges(1, 1):
        copy.wait_send()

    low_half = HALO // 2
    groups = (
        tuple(HALO + g * low_half for g in range(W)),
        (0, low_half, OWN - HALO, OWN - low_half),
    )
    lane = lax.broadcasted_iota(jnp.int32, (low_half, BS), 1)

    def boundary_half(h):
        at = pl.ds(h * low_half, low_half)
        return pltpu.make_async_remote_copy(
            src_ref=packed.at[at],
            dst_ref=arrived.at[at],
            send_sem=edge_sem.at[0, h],
            recv_sem=edge_sem.at[1, h],
            device_id=(after, row),
            device_id_type=MESH,
        )

    def send_boundary(h):
        strip = jnp.zeros((low_half, BS), F32)
        for g, first_row in enumerate(groups[h]):
            turned = pltpu.roll(ybuf[0, pl.ds(first_row, low_half)], (NB * (g + 1)) % BS, 1)
            strip = jnp.where(lane // NB == g, turned, strip)
        packed[pl.ds(h * low_half, low_half)] = strip.astype(BF16)
        boundary_half(h).start()

    def double(j, carry):
        turn = lax.rem(j + 1, 2)
        later = 1 - turn
        term = lax.rem(2 * j, DEG)
        scales = factors(term)

        @pl.when(j > 1)
        def _():
            for p in range(NP):
                low_ahead(later, p).wait_send()
                high_ahead(later, p).wait_send()

        own_part(0, 1, scales)
        ahead[1] = acc[1].astype(BF16)
        for p in range(NP):
            high_ahead(turn, p).start()
        ahead[0] = acc[0].astype(BF16)
        for p in range(NP):
            low_ahead(turn, p).start()
        inner(0, 1, term, scales)
        early[1] = dot(dense[QUADS - 1, :, :HALO], vbuf[1, pl.ds(OWN - 2 * HALO, HALO)])
        early[0] = dot(dense[0, :, 2 * HALO :], vbuf[1, pl.ds(HALO, HALO)])

        @pl.when(j == 1)
        def _():
            for parity, mine in halves:
                other = halves[1 - parity][1]

                @pl.when(lax.rem(cut, 2) == parity)
                def _(mine=mine, other=other):
                    for side in (0, 1):
                        for i in mine:
                            swapped(side, i).wait_send()
                        for i in other:
                            swapped(side, i).wait_recv()

        known[1] = scales[0] * dot(corner[1], vbuf[0, bottom])
        known[0] = scales[0] * dot(corner[0], vbuf[0, top])
        for p in range(NP):
            low_edge(0, turn, p).wait_recv()
        product = dot(dense[QUADS - 1, :, 2 * HALO :], halo[turn, 1])
        settle(1, bottom, acc[1] + scales[0] * product, term)
        scales = factors(term + 1)
        product = early[1] + dot(dense[QUADS - 1, :, HALO : 2 * HALO], vbuf[1, bottom])
        acc[1] = recur(1, 0, bottom, product, scales)
        for p in range(NP):
            high_edge(0, turn, p).wait_recv()
        product = dot(dense[0, :, :HALO], halo[turn, 0])
        settle(1, top, acc[0] + factors(term)[0] * product, term)
        product = early[0] + dot(dense[0, :, HALO : 2 * HALO], vbuf[1, top])
        acc[0] = recur(1, 0, top, product, scales)
        for copy in edges(0, turn):
            copy.wait_send()
        more = j < ROUNDS - 1

        inner(1, 0, term + 1, scales)

        @pl.when(jnp.logical_not(more))
        def _():
            send_boundary(0)

        for p in range(NP):
            low_ahead(turn, p).wait_recv()
            at = pl.ds(p * PIECE, PIECE)
            middle[1, at] = (fetched[turn, 1, at].astype(F32) + known[1, at]).astype(BF16)
            rows = pl.ds(OWN - HALO + p * PIECE, PIECE)
            settle(0, rows, bottom_piece(middle.at[1], p, scales), term + 1)

            @pl.when(more)
            def _(p=p):
                high_edge(0, later, p).start()

        for p in range(NP):
            high_ahead(turn, p).wait_recv()
            at = pl.ds(p * PIECE, PIECE)
            middle[0, at] = (fetched[turn, 0, at].astype(F32) + known[0, at]).astype(BF16)
        for p in range(NP):
            settle(0, pl.ds(p * PIECE, PIECE), top_piece(middle.at[0], p, scales), term + 1)

            @pl.when(more)
            def _(p=p):
                low_edge(0, later, p).start()

        return carry

    lax.fori_loop(1, ROUNDS, double, 0)
    for p in range(NP):
        low_ahead(ROUNDS % 2, p).wait_send()
        high_ahead(ROUNDS % 2, p).wait_send()
    last = 0

    send_boundary(1)
    square = jnp.zeros((BS, BS), F32)
    cross = jnp.zeros((NB, BS), F32)
    for h in (0, 1):
        boundary_half(h).wait()
        at = pl.ds(h * low_half, low_half)

        @pl.when(cut == 0)
        def _(at=at):
            arrived[at] = jnp.zeros((low_half, BS), BF16)

        boundary = arrived[at]
        square = square + tdot(boundary, boundary)
        for g, first_row in enumerate(groups[h]):
            mine = vbuf[last, pl.ds(first_row, low_half)]
            cross = cross + tdot(boundary, mine)[g * NB : (g + 1) * NB]

    def share(src, slots, sent, got, peers):
        copies = []
        for o, peer in enumerate(peers):
            copies.append(
                pltpu.make_async_remote_copy(
                    src_ref=src,
                    dst_ref=slots.at[o],
                    send_sem=sent.at[o],
                    recv_sem=got.at[o],
                    device_id=(cut, peer),
                    device_id_type=MESH,
                )
            )
            copies[-1].start()
        return copies

    def collect(copies, own, slots):
        summed = own
        for o, copy in enumerate(copies):
            copy.wait()
            summed = summed + slots[o]
        return summed

    eight = BS // W // W
    group = lax.broadcasted_iota(jnp.int32, (eight, BS), 1) // NB
    gram = jnp.zeros((NB, BS), F32)
    for g in range(W):
        rows = square[g * NB : (g + 1) * NB]
        gram = gram + (pltpu.roll(rows, (BS - NB * g) % BS, 1) if g else rows)
    tight = jnp.zeros((eight, BS), F32)
    for g in range(W):
        rows = gram[g * eight : (g + 1) * eight]
        tight = jnp.where(group == g, pltpu.roll(rows, NB * g, 1) if g else rows, tight)
    gpart[...] = tight
    gram_z = share(gpart, gzin, gzsend, gzrecv, zpeers)
    cpart[...] = cross
    cross_z = share(cpart, czin, czsend, czrecv, zpeers)
    gmid[...] = collect(gram_z, tight, gzin)
    gram_x = share(gmid, gxin, gxsend, gxrecv, xpeers)
    cmid[...] = collect(cross_z, cross, czin)
    cross_x = share(cmid, cxin, cxsend, cxrecv, xpeers)
    tight = collect(gram_x, gmid[...], gxin)

    across = lax.broadcasted_iota(jnp.int32, (NB, BS), 1)
    down = lax.broadcasted_iota(jnp.int32, (NB, BS), 0)
    loose = [tight if g == 0 else pltpu.roll(tight, BS - NB * g, 1) for g in range(W)]
    whole = jnp.where(across < NB, jnp.concatenate(loose, axis=0), 0.0)
    whole = whole + jnp.where((across == down) | (across == down + NB), 1.0, 0.0)
    for j in range(NB):
        row_j = whole[j : j + 1] * (1.0 / whole[j : j + 1, j : j + 1])
        whole = jnp.where(down == j, row_j, whole - whole[:, j : j + 1] * row_j)
    summed = collect(cross_x, cmid[...], cxin)
    tall = jnp.concatenate(
        [jnp.zeros((NB, BS), F32), summed, jnp.zeros((2 * NB, BS), F32)], axis=0
    )
    right = jnp.dot(whole, tall, preferred_element_type=F32, precision=lax.Precision.HIGHEST)
    solved = right.astype(BF16).astype(F32)
    for g in range(W):
        above_rows = [jnp.zeros((NB, BS), F32)] * g
        below_rows = [jnp.zeros((NB, BS), F32)] * (W - 1 - g)
        spread = jnp.concatenate([*above_rows, solved, *below_rows], axis=0).astype(BF16)
        for h in (0, 1):
            correction = dot(arrived[pl.ds(h * low_half, low_half)], spread)
            rows = pl.ds(groups[h][g], low_half)
            out[rows] = (ybuf[last, rows] - correction).astype(BF16)


def body(nz, nx, ncut, vectors, blocks, block_cols, counts, lower_end, upper_end, coeffs):
    blocks = blocks.reshape(RB * MAXB, BS, BS)
    hbm = pl.BlockSpec(memory_space=pltpu.HBM)
    stage = pltpu.VMEM((W * MAXB + 1, BS, BS), BF16)
    dma = pltpu.SemaphoreType.DMA
    return pl.pallas_call(
        functools.partial(kernel, nz, nx, ncut),
        out_shape=pltpu.VMEM((OWN, BS), BF16),
        in_specs=[hbm] * 7,
        out_specs=pl.BlockSpec(memory_space=pltpu.VMEM),
        scratch_shapes=[
            pltpu.SMEM((MAXB, RB), jnp.int32),
            pltpu.SMEM((RB,), jnp.int32),
            pltpu.SMEM((1,), F32),
            pltpu.SMEM((1,), F32),
            pltpu.SMEM((1, DEG + 1), F32),
            stage,
            stage,
            stage,
            stage,
            pltpu.VMEM((QUADS, HALO, WIDE), BF16),
            pltpu.VMEM((2, OWN, BS), BF16),
            pltpu.VMEM((2, OWN, BS), F32),
            pltpu.VMEM((OWN, BS), F32),
            pltpu.VMEM((OWN, BS), BF16),
            pltpu.VMEM((HALO, BS), BF16),
            pltpu.VMEM((HALO, BS), BF16),
            pltpu.VMEM((2, HALO, BS), F32),
            pltpu.VMEM((2, 2, HALO, BS), BF16),
            pltpu.VMEM((2, HALO, BS), BF16),
            pltpu.VMEM((2, 2, HALO, BS), BF16),
            pltpu.VMEM((2, HALO, BS), F32),
            pltpu.VMEM((2, HALO, BS), F32),
            pltpu.VMEM((2, HALO, BS), BF16),
            pltpu.VMEM((2, HALO, HALO), BF16),
            pltpu.VMEM((8, BS), F32),
            pltpu.VMEM((nz - 1, 8, BS), F32),
            pltpu.VMEM((8, BS), F32),
            pltpu.VMEM((nx - 1, 8, BS), F32),
            pltpu.VMEM((NB, BS), F32),
            pltpu.VMEM((nz - 1, NB, BS), F32),
            pltpu.VMEM((NB, BS), F32),
            pltpu.VMEM((nx - 1, NB, BS), F32),
            dma((5,)),
            dma((QUADS,)),
            dma,
            *[dma((2, 2, NP))] * 4,
            *[dma((2, W))] * 4,
            dma((2, 2)),
            *[dma((n,)) for n in 2 * [nz - 1, nz - 1, nx - 1, nx - 1]],
        ],
        compiler_params=pltpu.CompilerParams(
            collective_id=0, has_side_effects=True, vmem_limit_bytes=59 * 1024 * 1024
        ),
    )(vectors, blocks, block_cols.T, counts, lower_end, upper_end, coeffs)


def solution(mesh):
    rows = mesh.shape["rows"]
    nx = 4 if rows == 32 else 2
    return jax.shard_map(
        functools.partial(body, rows // nx, nx, mesh.shape["cuts"]),
        mesh=mesh,
        in_specs=(
            P("rows", "cuts"),
            P("rows", None, None, None),
            P("rows", None),
            P("rows"),
            P("cuts"),
            P("cuts"),
            P("cuts", None),
        ),
        out_specs=P("rows", "cuts"),
        check_vma=False,
    )
```
